128 devices in a mesh: region: 128 (over z, x, y, core).
Axes of the slice: x: 4, y: 4, z: 4, core: 2. Of those that a mesh axis runs over, the one named last changes fastest.
Arguments:
- gaussians: float32 [128, 9, 4096], P('region')
- depth: int32 [128, 512, 8], P('region'), may hold values from 0 to 7, each once within a row
- coverage: int32 [128, 512], P('region'), may hold values 0 or 1
- flips: int32 [512, 127], replicated, may hold values 0 or 1
- features: bfloat16 [131072, 384], P('region'), may hold values from -6 to 6
- w_first: bfloat16 [384, 384], replicated, may hold values from -0.3125 to 0.3125
- b_first: float32 [384], replicated, may hold values from -3 to 3
- w_second: bfloat16 [384], replicated, may hold values from -0.3125 to 0.3125
- target: float32 [3, 131072], P(None, 'region'), may hold values from 0 to 1
Outputs:
- pixel_loss: float32 [131072], P('region')
- splat_grads: float32 [128, 9, 4096], P('region')
The draws below stay inside these ranges and needn't reach their ends.
Inputs may be any that keep to these rules, and one draw needn't show every extreme that they name: Each tile's 8 depth ranks of one region are a permutation of 0 to 7.
All inputs are finite; a program needn't handle non-finite values. No bound on the sum of `coverage` on one device may be relied on, other than what follows from the above.
Results may differ from the reference program's by a relative error of at most 0.0022.
Values sent between devices are 32-bit elements; how exact they have to be, the bound alone decides.
No kernel may reach another device: no remote copies, remote signals or barrier semaphores. Data moves between devices by JAX's collectives and lax.ppermute only.
A program may use at most 64 MiB of HBM per device.

```python
import math
import jax
import jax.numpy as jnp
from jax import lax

TILES = 512
TSIDE = 16
GPT = 8
FEAT = 384
HID = 384
REGIONS = 128
NODES = 127
PIXELS = 131072


def draw_gaussians(key, part):
    lower = jnp.array([-1.0, -1.0, 0.0, 0.0, -1.5, -4.0, -2.5, -2.5, -2.5], jnp.float32)
    upper = jnp.array([TSIDE + 1.0, TSIDE + 1.0, math.log(TSIDE * 0.5), math.log(TSIDE * 0.5), 1.5, 1.0, 2.5, 2.5, 2.5], jnp.float32)
    uniform_draw = jax.random.uniform(key, (REGIONS, 9, TILES * GPT), jnp.float32)
    return lower[None, :, None] + (upper - lower)[None, :, None] * uniform_draw


def with_ends(values, rng, smallest, high):
    index_at = [jax.random.randint(jax.random.fold_in(rng, axis), (), 0, length) for axis, length in enumerate(values.shape)]
    longest = values.shape.index(max(values.shape))
    next_to = index_at[:longest] + [(index_at[longest] + 1) % values.shape[longest]] + index_at[longest + 1:]
    return values.at[tuple(index_at)].set(smallest).at[tuple(next_to)].set(high)


def shard_levels(own_key, dims, cuts, smallest, high):
    def one(dim, parts):
        heights = jax.random.uniform(jax.random.fold_in(jax.random.fold_in(own_key, 6), dim), (parts,), jnp.float32, smallest / len(cuts), high / len(cuts))
        return jnp.repeat(jnp.exp(heights), dims[dim] // parts).reshape((-1,) + (1,) * (len(dims) - dim - 1))

    loudness = one(*cuts[0])
    for cut in cuts[1:]:
        loudness = loudness * one(*cut)
    return loudness


def normal_values(stream_key, dims, deviation, bound, split=(), dtype=jnp.bfloat16):
    entries = deviation * jax.random.normal(stream_key, dims, jnp.float32)
    if split:
        entries = entries * shard_levels(stream_key, dims, split, -0.22, 0.18)
    return jnp.clip(entries, -bound, bound).astype(dtype)


def setup_inputs(seed: int = 0) -> dict:
    key_list = jax.random.split(jax.random.key(seed), 10)
    gaussians = draw_gaussians(jax.random.fold_in(key_list[9], 71), 0)
    depth = jax.vmap(lambda own: jax.random.permutation(own, GPT))(jax.random.split(key_list[1], REGIONS * TILES)).reshape((REGIONS, TILES, GPT)).astype(jnp.int32)
    coverage = with_ends((jax.random.randint(key_list[2], (REGIONS, TILES), 0, 4) < 1).astype(jnp.int32), jax.random.fold_in(key_list[2], 1), 0, 1)
    flips = with_ends((jax.random.randint(key_list[3], (TILES, NODES), 0, 2) < 1).astype(jnp.int32), jax.random.fold_in(key_list[3], 1), 0, 1)
    features = normal_values(key_list[4], (PIXELS, FEAT), 1.0, 6.0, ((0, 128),))
    w_first = normal_values(key_list[5], (FEAT, HID), FEAT ** -0.5, 0.3125)
    b_first = normal_values(key_list[6], (HID,), 0.5, 3.0, (), jnp.float32)
    w_second = normal_values(key_list[7], (HID,), HID ** -0.5, 0.3125)
    target = jnp.clip(1.0 * jax.random.uniform(key_list[8], (3, PIXELS), jnp.float32) ** shard_levels(key_list[8], (3, PIXELS), ((1, 128),), -0.2, 0.2), 0.0, 1.0)
    return {"gaussians": gaussians, "depth": depth, "coverage": coverage, "flips": flips, "features": features, "w_first": w_first, "b_first": b_first, "w_second": w_second, "target": target}


def render_tiles(params, splat_ranks, covered):
    pixel_index = jnp.arange(TSIDE * TSIDE)
    column_pos = (pixel_index % TSIDE).astype(jnp.float32) + 0.5
    row_pos = (pixel_index // TSIDE).astype(jnp.float32) + 0.5
    delta_x = column_pos[None, None, :] - params[0][:, :, None]
    delta_y = row_pos[None, None, :] - params[1][:, :, None]
    unit_x = delta_x * jnp.exp(-params[2])[:, :, None]
    unit_y = delta_y * jnp.exp(-params[3])[:, :, None]
    correlation = (0.9 * jnp.tanh(params[4]))[:, :, None]
    quadratic = (unit_x * unit_x - 2.0 * correlation * unit_x * unit_y + unit_y * unit_y) / (1.0 - correlation * correlation)
    opacity = 0.99 * jax.nn.sigmoid(params[5]) * covered[:, None].astype(jnp.float32)
    absorb = opacity[:, :, None] * jnp.exp(-0.5 * quadratic)
    log_trans = jnp.log1p(-absorb)
    prior = (splat_ranks[:, None, :] < splat_ranks[:, :, None]).astype(jnp.float32)
    leading = jnp.einsum('tgh,thp->tgp', prior, log_trans, precision=lax.Precision.HIGHEST)
    weight = jnp.exp(leading) * absorb
    colors = jax.nn.sigmoid(params[6:9])
    color_sum = lax.optimization_barrier(jnp.sum(colors[:, :, :, None] * weight[None], 2))
    transmit = jnp.exp(lax.optimization_barrier(jnp.sum(log_trans, axis=1)))
    return jnp.concatenate([color_sum, transmit[None]], 0)

def over_pair(front_layer, back_layer):
    blended = front_layer[:, :3] + front_layer[:, 3:4] * back_layer[:, :3]
    transmit = front_layer[:, 3:4] * back_layer[:, 3:4]
    return jnp.concatenate([blended, transmit], 1)

def tree_levels(stack, stripe_flips):
    number = stack.shape[0]
    while number > 1:
        half_count = number // 2
        in_front = (stripe_flips[:, half_count - 1:2 * half_count - 1].T > 0)[:, None, :, None]
        paired = stack.reshape((half_count, 2) + stack.shape[1:])
        front_layer = jnp.where(in_front, paired[:, 1], paired[:, 0])
        back_layer = jnp.where(in_front, paired[:, 0], paired[:, 1])
        stack = over_pair(front_layer, back_layer)
        number = half_count
    return stack[0]

def uncertainty(stripe_feats, w_first, b_first, w_second):
    hidden = jax.nn.gelu(jnp.dot(stripe_feats, w_first, preferred_element_type=jnp.float32) + b_first).astype(jnp.bfloat16)
    return 0.5 + jax.nn.softplus(jnp.dot(hidden, w_second, preferred_element_type=jnp.float32))

def reference(gaussians, depth, coverage, flips, features, w_first, b_first, w_second, target):
    regions = gaussians.shape[0]
    tile_count = depth.shape[1]
    splats = depth.shape[2]
    stripe_tiles = tile_count // regions
    tile_pixels = TSIDE * TSIDE
    grid_params = gaussians.reshape(regions, 9, tile_count, splats)

    def stripe_work(stripe_index):
        first_tile = (stripe_index * stripe_tiles).astype(jnp.int32)
        params = lax.dynamic_slice_in_dim(grid_params, first_tile, stripe_tiles, 2)
        splat_ranks = lax.dynamic_slice_in_dim(depth, first_tile, stripe_tiles, 1)
        covered = lax.dynamic_slice_in_dim(coverage, first_tile, stripe_tiles, 1)
        stripe_flips = lax.dynamic_slice_in_dim(flips, first_tile, stripe_tiles, 0)
        first_pixel = (first_tile * tile_pixels).astype(jnp.int32)
        stripe_feats = lax.dynamic_slice_in_dim(features, first_pixel, stripe_tiles * tile_pixels, 0)
        wanted = lax.dynamic_slice_in_dim(target, first_pixel, stripe_tiles * tile_pixels, 1).reshape(3, stripe_tiles, tile_pixels)
        spread = uncertainty(stripe_feats, w_first, b_first, w_second).reshape(stripe_tiles, tile_pixels)

        def stripe_loss(region_params):
            pieces = jax.vmap(render_tiles)(region_params, splat_ranks, covered)
            composite = tree_levels(pieces, stripe_flips)
            residual = composite[:3] + composite[3:4] - wanted
            return lax.optimization_barrier(jnp.sum(residual * residual, 0)) / (2.0 * spread * spread)
        loss_part, pull_back = jax.vjp(stripe_loss, params)
        gradient, = pull_back(jnp.ones_like(loss_part))
        return (loss_part + jnp.log(spread), gradient)
    losses, gradients = lax.map(stripe_work, jnp.arange(regions).astype(jnp.int32))
    pixel_loss = losses.reshape(tile_count * tile_pixels)
    splat_grads = gradients.transpose(1, 2, 0, 3, 4).reshape(regions, 9, tile_count * splats)
    return (pixel_loss, splat_grads)
```

```python
import math

import jax
import jax.numpy as jnp
import numpy as np
from jax import lax
from jax.experimental import pallas as pl
from jax.experimental.pallas import tpu as pltpu
from jax.sharding import PartitionSpec as P

TSIDE = 16
PIX = TSIDE * TSIDE
SPLATS = 8
LANES = 128
WIDTH = 384
HALF_LOG2E = 0.5 * math.log2(math.e)
F32 = jnp.float32
BF16 = jnp.bfloat16


def cut_columns(source, shift):
    return pltpu.roll(source, shift, 1) if shift else source


def pack_kernel(gauss_ref, depth_ref, cover_ref, out_ref, turned, strided):
    group = lax.broadcasted_iota(jnp.int32, (32, LANES), 1) // 32
    for part in range(3):
        for d in range(4):
            block = None
            for a in range(min(4, 9 - 4 * part)):
                moved = cut_columns(gauss_ref[4 * part + a], 32 * ((a - d) % 4))
                block = moved if block is None else jnp.where(group == a, moved, block)
            strided[part, pl.ds(d, 32, stride=4), :] = block
    ranks = depth_ref[...].astype(F32)
    covered = cover_ref[...].astype(F32)
    filler = jnp.zeros((LANES - 16, 512), F32)
    row = lax.broadcasted_iota(jnp.int32, (8, 512), 0)
    covered = jnp.where(row == 0, jnp.broadcast_to(covered, (8, 512)), 0.0)
    stacked = jnp.concatenate([ranks, covered, filler], 0)
    for b in range(4):
        turned[pl.ds(b * LANES, LANES), :] = stacked[:, b * LANES : (b + 1) * LANES].T
    tail = None
    for t in range(4):
        moved = pltpu.roll(turned[pl.ds(t, LANES, stride=4), :], 32 + 16 * t, 1)
        tail = moved if tail is None else tail + moved
    lane = lax.broadcasted_iota(jnp.int32, (LANES, LANES), 1)
    out_ref[:, 0:128] = strided[0]
    out_ref[:, 128:256] = strided[1]
    out_ref[:, 256:384] = jnp.where(lane < 32, strided[2], tail)


def unpack_kernel(msg_ref, out_ref, strided):
    group = lax.broadcasted_iota(jnp.int32, (32, LANES), 1) // 32
    for part in range(3):
        strided[part] = msg_ref[:, part * LANES : (part + 1) * LANES]
    for p in range(9):
        a, part = p % 4, p // 4
        block = None
        for d in range(4):
            moved = cut_columns(strided[part, pl.ds(d, 32, stride=4), :], 32 * ((d - a) % 4))
            block = moved if block is None else jnp.where(group == d, moved, block)
        out_ref[p] = block


def pixel_kernel(feat_ref, w_first_ref, b_first_ref, w_second_ref, target_ref, pix_ref):
    pre = jnp.dot(feat_ref[...], w_first_ref[...], preferred_element_type=F32) + b_first_ref[...]
    hidden = jax.nn.gelu(pre).astype(BF16)
    rows = jnp.broadcast_to(w_second_ref[...], (LANES, w_second_ref.shape[1]))
    score = lax.dot_general(hidden, rows, (((1,), (1,)), ((), ())), preferred_element_type=F32)
    spread = 0.5 + (jnp.maximum(score, 0.0) + jnp.log1p(jnp.exp(-jnp.abs(score))))
    filler = jnp.zeros((LANES - 3, PIX), F32)
    wanted = jnp.concatenate([target_ref[...], filler], 0).T
    lane = lax.broadcasted_iota(jnp.int32, (PIX, LANES), 1)
    pix_ref[...] = jnp.where(
        lane == 3, 1.0 / (spread * spread), jnp.where(lane == 4, jnp.log(spread), wanted)
    )


def split_dot(value, matrix):
    high = value.astype(BF16)
    low = (value - high.astype(F32)).astype(BF16)
    return jnp.dot(high, matrix, preferred_element_type=F32) + jnp.dot(
        low, matrix, preferred_element_type=F32
    )


ROWS = 4
STEPS = TSIDE // ROWS


def splat_kernel(
    msg_ref, pix_ref, before_ref, behind_ref, loss_ref, out_ref,
    turned, rows, across, alphas, weights, clear, color, carry, sums, grads,
):
    for b in range(3):
        turned[pl.ds(b * LANES, LANES), :] = msg_ref[:, b * LANES : (b + 1) * LANES].T
    sub = lax.broadcasted_iota(jnp.int32, (8, LANES), 0).astype(F32)
    eye = lax.broadcasted_iota(jnp.int32, (LANES, LANES), 0) == lax.broadcasted_iota(
        jnp.int32, (LANES, LANES), 1
    )

    def tile(t, unused):
        def raw(p):
            return turned[pl.ds(pl.multiple_of(32 * p + 8 * t, 8), 8), :]

        ranks = turned[pl.ds(pl.multiple_of(288 + 16 * t, 8), 8), :]
        covered = turned[pl.ds(288 + 16 * t + 8, 1), :]
        inv_x = jnp.exp(-raw(2))
        inv_y = jnp.exp(-raw(3))
        curl = jnp.tanh(raw(4))
        rho = 0.9 * curl
        inv_det = 1.0 / (1.0 - rho * rho)
        scale = jnp.sqrt(HALF_LOG2E * inv_det)
        odds = jax.nn.sigmoid(raw(5))
        tint = [jax.nn.sigmoid(raw(6 + c)) for c in range(3)]
        plain = [raw(0), raw(1), inv_x * scale, inv_y * scale, 2.0 * rho, 0.99 * odds * covered] + tint

        for k in range(SPLATS):
            chosen = ranks == float(k)
            for n, value in enumerate(plain):
                row = jnp.sum(jnp.where(chosen, value, 0.0), axis=0, keepdims=True)
                rows[k * 9 + n] = jnp.broadcast_to(row, (8, LANES))
            for h in range(2):
                unit = (sub + (0.5 + 8.0 * h) - rows[k * 9]) * rows[k * 9 + 2]
                across[k, h, 0] = unit
                across[k, h, 1] = unit * rows[k * 9 + 4]
                across[k, h, 2] = unit * unit

        def unit_y(k, r, step):
            at = (step * ROWS + r).astype(F32) + 0.5
            return (at - rows[k * 9 + 1]) * rows[k * 9 + 3]

        def render(step, unused):
            trans = [[None] * 2 for _ in range(ROWS)]
            total = [[[None] * 3 for _ in range(2)] for _ in range(ROWS)]
            for k in range(SPLATS):
                opacity = rows[k * 9 + 5]
                shade = [rows[k * 9 + 6 + c] for c in range(3)]
                for r in range(ROWS):
                    down = unit_y(k, r, step)
                    for h in range(2):
                        power = down * (across[k, h, 1] - down) - across[k, h, 2]
                        alpha = opacity * jnp.exp2(power)
                        weight = alpha if k == 0 else trans[r][h] * alpha
                        trans[r][h] = 1.0 - alpha if k == 0 else trans[r][h] - weight
                        alphas[step, k, 2 * r + h] = alpha
                        weights[step, k, 2 * r + h] = weight
                        for c in range(3):
                            term = weight * shade[c]
                            total[r][h][c] = term if k == 0 else total[r][h][c] + term
            for r in range(ROWS):
                for h in range(2):
                    at = pl.ds(pl.multiple_of((step * ROWS + r) * 16 + 8 * h, 8), 8)
                    clear[at, :] = trans[r][h]
                    for c in range(3):
                        color[c, at, :] = total[r][h][c]
            return 0

        lax.fori_loop(0, STEPS, render, 0)

        through = clear[...]
        logs = split_dot(jnp.log(through), before_ref[t])
        ahead = jnp.exp(logs[:, :LANES])
        whole = jnp.exp(logs[:, LANES:])
        pix = pix_ref[pl.ds(pl.multiple_of(t * PIX, PIX), PIX), :]
        inv_square = jnp.broadcast_to(pix[:, 3:4], (PIX, LANES))
        ones = jnp.ones((LANES, LANES), BF16)
        squares = None
        grad_trans = None
        along = None
        for c in range(3):
            layer = ahead * color[c]
            residual = split_dot(layer, ones) + whole - pix[:, c : c + 1]
            slope = residual * inv_square
            squares = residual * residual if c == 0 else squares + residual * residual
            grad_trans = slope if c == 0 else grad_trans + slope
            along = slope * layer if c == 0 else along + slope * layer
            color[c] = ahead * slope
        loss = 0.5 * squares * inv_square + pix[:, 4:5]
        for h in range(2):
            line = jnp.where(eye, loss[h * LANES : (h + 1) * LANES], 0.0)
            loss_ref[pl.ds(2 * t + h, 1), :] = jnp.sum(line, axis=0, keepdims=True)
        follow = split_dot(along, behind_ref[t]) + grad_trans * whole
        carry[...] = follow / through

        sums[...] = jnp.zeros_like(sums)

        def pull(step, unused):
            behind = [None] * (2 * ROWS)
            slope = [[None] * 3 for _ in range(2 * ROWS)]
            for n in range(2 * ROWS):
                at = pl.ds(pl.multiple_of(step * (ROWS * 16) + 8 * n, 8), 8)
                behind[n] = carry[at, :]
                slope[n] = [color[c, at, :] for c in range(3)]
            for k in range(SPLATS - 1, -1, -1):
                shade = [rows[k * 9 + 6 + c] for c in range(3)]
                acc = [None] * 9

                def add(n, value):
                    acc[n] = value if acc[n] is None else acc[n] + value

                for r in range(ROWS):
                    down = unit_y(k, r, step)
                    for h in range(2):
                        n = 2 * r + h
                        alpha = alphas[step, k, n]
                        weight = weights[step, k, n]
                        gain = slope[n][0] * shade[0] + slope[n][1] * shade[1] + slope[n][2] * shade[2]
                        change = gain - behind[n]
                        behind[n] = behind[n] + alpha * change
                        pulled = weight * change
                        leaned = pulled * down
                        add(3 * h, pulled)
                        add(3 * h + 1, leaned)
                        add(3 * h + 2, leaned * down)
                        for c in range(3):
                            add(6 + c, weight * slope[n][c])
                for n in range(9):
                    sums[k * 9 + n] = sums[k * 9 + n] + acc[n]
            return 0

        lax.fori_loop(0, STEPS, pull, 0)

        plain_sums = [None] * 9
        for k in range(SPLATS):
            chosen = ranks == float(k)
            left, right = [[sums[k * 9 + 3 * h + n] for n in range(3)] for h in range(2)]
            u0, u1 = across[k, 0, 0], across[k, 1, 0]
            m0, m1 = left[0] * u0, right[0] * u1
            moments = [
                left[0] + right[0],
                m0 + m1,
                left[1] + right[1],
                m0 * u0 + m1 * u1,
                left[1] * u0 + right[1] * u1,
                left[2] + right[2],
            ] + [sums[k * 9 + 6 + c] for c in range(3)]
            for n, value in enumerate(moments):
                line = jnp.broadcast_to(jnp.sum(value, axis=0, keepdims=True), (8, LANES))
                plain_sums[n] = (
                    jnp.where(chosen, line, 0.0) if k == 0 else jnp.where(chosen, line, plain_sums[n])
                )
        s0, su, sv, suu, suv, svv = plain_sums[:6]
        inv_scale = 1.0 / scale
        su, sv = su * inv_scale, sv * inv_scale
        inv_both = inv_scale * inv_scale
        suu, suv, svv = suu * inv_both, suv * inv_both, svv * inv_both
        result = [
            inv_det * inv_x * (su - rho * sv),
            inv_det * inv_y * (sv - rho * su),
            inv_det * (suu - rho * suv),
            inv_det * (svv - rho * suv),
            inv_det
            * (suv - rho * inv_det * (suu - 2.0 * rho * suv + svv))
            * (0.9 * (1.0 - curl * curl)),
            s0 * (1.0 - odds),
        ] + [plain_sums[6 + c] * tint[c] * (1.0 - tint[c]) for c in range(3)]
        for p in range(9):
            grads[pl.ds(pl.multiple_of(32 * p + 8 * t, 8), 8), :] = result[p]
        return 0

    grads[pl.ds(288, 96), :] = jnp.zeros((96, LANES), F32)
    lax.fori_loop(0, 4, tile, 0)
    for b in range(3):
        out_ref[:, b * LANES : (b + 1) * LANES] = grads[pl.ds(b * LANES, LANES), :].T


def order_matrix(regions):
    levels = regions.bit_length() - 1
    turns = np.zeros((regions - 1, regions), np.float32)
    for r in range(regions):
        for d in range(levels):
            bit = (r >> (levels - 1 - d)) & 1
            turns[2**d - 1 + (r >> (levels - d)), r] = (1 - 2 * bit) * 2 ** (levels - 1 - d)
    return turns


def vmem(*shape, dtype=F32):
    return pltpu.VMEM(shape, dtype)


def shards(gaussians, depth, coverage, flips, features, w_first, b_first, w_second, target):
    regions = lax.axis_size("region")
    my_index = lax.axis_index("region")
    limit = pltpu.CompilerParams(vmem_limit_bytes=32 * 1024 * 1024)

    message = pl.pallas_call(
        pack_kernel,
        out_shape=jax.ShapeDtypeStruct((regions, WIDTH), F32),
        scratch_shapes=[vmem(512, LANES), vmem(3, LANES, LANES)],
        compiler_params=limit,
        name="pack",
    )(gaussians.reshape(9, 32, LANES), depth[0].T, coverage)
    received = lax.all_to_all(message, "region", 0, 0, tiled=True)

    pix = pl.pallas_call(
        pixel_kernel,
        grid=(4,),
        in_specs=[
            pl.BlockSpec((PIX, 384), lambda i: (i, 0)),
            pl.BlockSpec((384, 384), lambda i: (0, 0)),
            pl.BlockSpec((1, 384), lambda i: (0, 0)),
            pl.BlockSpec((1, 384), lambda i: (0, 0)),
            pl.BlockSpec((3, PIX), lambda i: (0, i)),
        ],
        out_specs=pl.BlockSpec((PIX, LANES), lambda i: (i, 0)),
        out_shape=jax.ShapeDtypeStruct((4 * PIX, LANES), F32),
        compiler_params=limit,
        cost_estimate=pl.CostEstimate(
            flops=2 * 1024 * 384 * 512, bytes_accessed=2_000_000, transcendentals=1024 * 384
        ),
        name="pixels",
    )(features, w_first, b_first[None], w_second[None], target)

    my_flips = lax.dynamic_slice_in_dim(flips, my_index * 4, 4, 0).astype(F32)
    turned = jnp.dot(my_flips, jnp.asarray(order_matrix(regions)), precision=lax.Precision.HIGHEST)
    rank = jnp.arange(regions, dtype=F32)[None] + turned
    before = (rank[:, :, None] < rank[:, None, :]).astype(BF16)
    behind = (rank[:, :, None] > rank[:, None, :]).astype(BF16)
    before = jnp.concatenate([before, jnp.ones_like(before)], 2)

    loss, returned = pl.pallas_call(
        splat_kernel,
        out_shape=(
            jax.ShapeDtypeStruct((8, LANES), F32),
            jax.ShapeDtypeStruct((regions, WIDTH), F32),
        ),
        scratch_shapes=[
            vmem(WIDTH, LANES),
            vmem(72, 8, LANES),
            vmem(SPLATS, 2, 3, 8, LANES),
            vmem(STEPS, SPLATS, 2 * ROWS, 8, LANES),
            vmem(STEPS, SPLATS, 2 * ROWS, 8, LANES),
            vmem(PIX, LANES),
            vmem(3, PIX, LANES),
            vmem(PIX, LANES),
            vmem(72, 8, LANES),
            vmem(WIDTH, LANES),
        ],
        compiler_params=limit,
        name="splats",
    )(received, pix, before, behind)

    back = lax.all_to_all(returned, "region", 0, 0, tiled=True)
    splat_grads = pl.pallas_call(
        unpack_kernel,
        out_shape=jax.ShapeDtypeStruct((9, 32, LANES), F32),
        scratch_shapes=[vmem(3, LANES, LANES)],
        compiler_params=limit,
        name="unpack",
    )(back)
    return loss.reshape(4 * PIX), splat_grads.reshape(1, 9, 32 * LANES)


def solution(mesh):
    placed = (
        P("region", None, None),
        P("region", None, None),
        P("region", None),
        P(),
        P("region", None),
        P(),
        P(),
        P(),
        P(None, "region"),
    )
    return jax.shard_map(
        shards,
        mesh=mesh,
        in_specs=placed,
        out_specs=(P("region"), P("region", None, None)),
        check_vma=False,
    )
```

```python
import math

import jax
import jax.numpy as jnp
import numpy as np
from jax import lax
from jax.experimental import pallas as pl
from jax.experimental.pallas import tpu as pltpu
from jax.sharding import PartitionSpec as P

TSIDE = 16
PIX = TSIDE * TSIDE
SPLATS = 8
LANES = 128
WIDTH = 384
HALF_LOG2E = 0.5 * math.log2(math.e)
F32 = jnp.float32
BF16 = jnp.bfloat16


def cut_columns(source, shift):
    return pltpu.roll(source, shift, 1) if shift else source


def pack_kernel(gauss_ref, depth_ref, cover_ref, out_ref, turned, strided):
    group = lax.broadcasted_iota(jnp.int32, (32, LANES), 1) // 32
    for part in range(3):
        for d in range(4):
            block = None
            for a in range(min(4, 9 - 4 * part)):
                moved = cut_columns(gauss_ref[4 * part + a], 32 * ((a - d) % 4))
                block = moved if block is None else jnp.where(group == a, moved, block)
            if part < 2:
                out_ref[pl.ds(3 * d + part, 32, stride=12), :] = block
            else:
                strided[pl.ds(d, 32, stride=4), :] = block
    ranks = depth_ref[...].astype(F32)
    covered = cover_ref[...].astype(F32)
    filler = jnp.zeros((LANES - 16, 512), F32)
    row = lax.broadcasted_iota(jnp.int32, (8, 512), 0)
    covered = jnp.where(row == 0, jnp.broadcast_to(covered, (8, 512)), 0.0)
    stacked = jnp.concatenate([ranks, covered, filler], 0)
    for b in range(4):
        turned[pl.ds(b * LANES, LANES), :] = stacked[:, b * LANES : (b + 1) * LANES].T
    tail = None
    for t in range(4):
        moved = pltpu.roll(turned[pl.ds(t, LANES, stride=4), :], 32 + 16 * t, 1)
        tail = moved if tail is None else tail + moved
    lane = lax.broadcasted_iota(jnp.int32, (LANES, LANES), 1)
    out_ref[pl.ds(2, LANES, stride=3), :] = jnp.where(lane < 32, strided[...], tail)


def unpack_kernel(msg_ref, out_ref):
    group = lax.broadcasted_iota(jnp.int32, (32, LANES), 1) // 32
    for p in range(9):
        a, part = p % 4, p // 4
        block = None
        for d in range(4):
            moved = cut_columns(msg_ref[pl.ds(3 * d + part, 32, stride=12), :], 32 * ((d - a) % 4))
            block = moved if block is None else jnp.where(group == d, moved, block)
        out_ref[p] = block


def pixel_kernel(feat_ref, w_first_ref, b_first_ref, w_second_ref, target_ref, pix_ref):
    pre = jnp.dot(feat_ref[...], w_first_ref[...], preferred_element_type=F32) + b_first_ref[...]
    hidden = jax.nn.gelu(pre).astype(BF16)
    rows = jnp.broadcast_to(w_second_ref[...], (LANES, w_second_ref.shape[1]))
    score = lax.dot_general(hidden, rows, (((1,), (1,)), ((), ())), preferred_element_type=F32)
    spread = 0.5 + (jnp.maximum(score, 0.0) + jnp.log1p(jnp.exp(-jnp.abs(score))))
    filler = jnp.zeros((LANES - 3, PIX), F32)
    wanted = jnp.concatenate([target_ref[...], filler], 0).T
    lane = lax.broadcasted_iota(jnp.int32, (PIX, LANES), 1)
    pix_ref[...] = jnp.where(
        lane == 3, 1.0 / (spread * spread), jnp.where(lane == 4, jnp.log(spread), wanted)
    )


def split_dot(value, matrix):
    high = value.astype(BF16)
    low = (value - high.astype(F32)).astype(BF16)
    return jnp.dot(high, matrix, preferred_element_type=F32) + jnp.dot(
        low, matrix, preferred_element_type=F32
    )


ROWS = 4
STEPS = TSIDE // ROWS


def splat_kernel(
    msg_ref, pix_ref, before_ref, behind_ref, loss_ref, out_ref,
    turned, places, sources, rows, across, alphas, weights, clear, color, carry, sums, grads,
):
    for b in range(3):
        turned[pl.ds(b * LANES, LANES), :] = msg_ref[pl.ds(b, LANES, stride=3), :].T
    sub = lax.broadcasted_iota(jnp.int32, (8, LANES), 0).astype(F32)
    lane = lax.broadcasted_iota(jnp.int32, (LANES, LANES), 1)
    line = lax.broadcasted_iota(jnp.int32, (LANES, LANES), 0)

    counts = []
    for t in range(4):
        kept = jnp.where(lane[:1] == 0, 1.0, turned[pl.ds(288 + 16 * t + 8, 1), :])
        counts.append(jnp.sum(kept).astype(jnp.int32))
        earlier = before_ref[t] if t % 2 == 0 else behind_ref[t]
        spot = jnp.dot(
            jnp.broadcast_to(kept, (8, LANES)).astype(BF16), earlier, preferred_element_type=F32
        )
        spot = spot if t % 2 == 0 else (LANES - 1.0) - spot
        spot = jnp.where(kept > 0.0, spot, -1.0).astype(jnp.int32)
        places[t] = spot
        hit = jnp.broadcast_to(spot[:1].astype(F32), (LANES, LANES)).T == lane.astype(F32)
        source = jnp.sum(jnp.where(hit, line.astype(F32), 0.0), axis=0, keepdims=True)
        sources[t] = jnp.broadcast_to(source, (8, LANES)).astype(jnp.int32)

    def block(i, unused):
        pair, second = i // 2, i % 2
        first_count = jnp.where(pair == 0, counts[0], counts[2])
        last_count = jnp.where(pair == 0, counts[1], counts[3])
        fits = first_count + last_count <= LANES
        has_first = jnp.logical_or(fits, second == 0)
        has_last = jnp.logical_or(fits, second == 1)
        border = jnp.where(has_first, jnp.where(has_last, first_count, LANES), 0)

        @pl.when(jnp.logical_not(jnp.logical_and(fits, second == 1)))
        def _():
            both_tiles(2 * pair, has_first, has_last, first_count, last_count, border)

        return 0

    def both_tiles(t, has_first, has_last, first_count, last_count, border):
        flat = lane[:8]
        in_first = flat < jnp.where(has_first, first_count, 0)
        in_last = flat >= jnp.where(has_last, LANES - last_count, LANES)
        first_source, last_source = sources[t], sources[t + 1]

        def pick(at, step):
            left = turned[pl.ds(pl.multiple_of(at, 8), 8), :]
            right = turned[pl.ds(pl.multiple_of(at + step, 8), 8), :]
            left = jnp.take_along_axis(left, first_source, axis=1)
            right = jnp.take_along_axis(right, last_source, axis=1)
            return jnp.where(in_first, left, jnp.where(in_last, right, 0.0))

        def raw(p):
            return pick(32 * p + 8 * t, 8)

        ranks = pick(288 + 16 * t, 16)
        covered = pick(288 + 16 * t + 8, 16)[:1]
        inv_x = jnp.exp(-raw(2))
        inv_y = jnp.exp(-raw(3))
        curl = jnp.tanh(raw(4))
        rho = 0.9 * curl
        inv_det = 1.0 / (1.0 - rho * rho)
        scale = jnp.sqrt(HALF_LOG2E * inv_det)
        odds = jax.nn.sigmoid(raw(5))
        tint = [jax.nn.sigmoid(raw(6 + c)) for c in range(3)]
        plain = [raw(0), raw(1), inv_x * scale, inv_y * scale, 2.0 * rho, 0.99 * odds * covered] + tint

        for k in range(SPLATS):
            chosen = ranks == float(k)
            for n, value in enumerate(plain):
                row = jnp.sum(jnp.where(chosen, value, 0.0), axis=0, keepdims=True)
                rows[k * 9 + n] = jnp.broadcast_to(row, (8, LANES))
            for h in range(2):
                unit = (sub + (0.5 + 8.0 * h) - rows[k * 9]) * rows[k * 9 + 2]
                across[k, h, 0] = unit
                across[k, h, 1] = unit * rows[k * 9 + 4]
                across[k, h, 2] = unit * unit

        def unit_y(k, r, step):
            at = (step * ROWS + r).astype(F32) + 0.5
            return (at - rows[k * 9 + 1]) * rows[k * 9 + 3]

        def render(step, unused):
            trans = [[None] * 2 for _ in range(ROWS)]
            total = [[[None] * 3 for _ in range(2)] for _ in range(ROWS)]
            for k in range(SPLATS):
                opacity = rows[k * 9 + 5]
                shade = [rows[k * 9 + 6 + c] for c in range(3)]
                for r in range(ROWS):
                    down = unit_y(k, r, step)
                    for h in range(2):
                        power = down * (across[k, h, 1] - down) - across[k, h, 2]
                        alpha = opacity * jnp.exp2(power)
                        weight = alpha if k == 0 else trans[r][h] * alpha
                        trans[r][h] = 1.0 - alpha if k == 0 else trans[r][h] - weight
                        alphas[step, k, 2 * r + h] = alpha
                        weights[step, k, 2 * r + h] = weight
                        for c in range(3):
                            term = weight * shade[c]
                            total[r][h][c] = term if k == 0 else total[r][h][c] + term
            for r in range(ROWS):
                for h in range(2):
                    at = pl.ds(pl.multiple_of((step * ROWS + r) * 16 + 8 * h, 8), 8)
                    clear[at, :] = trans[r][h]
                    for c in range(3):
                        color[c, at, :] = total[r][h][c]
            return 0

        lax.fori_loop(0, STEPS, render, 0)

        through = clear[...]
        same = (lane < border) == (line < border)
        to_left = jnp.where(jnp.logical_and(same, line < lane), 1.0, 0.0).astype(BF16)
        to_right = jnp.where(jnp.logical_and(same, line > lane), 1.0, 0.0).astype(BF16)
        same = jnp.where(same, 1.0, 0.0).astype(BF16)
        logs = split_dot(jnp.log(through), jnp.concatenate([to_left, same], 1))
        ahead = jnp.exp(logs[:, :LANES])
        whole = jnp.exp(logs[:, LANES:])
        left_pix = pix_ref[pl.ds(pl.multiple_of(t * PIX, PIX), PIX), :]
        right_pix = pix_ref[pl.ds(pl.multiple_of((t + 1) * PIX, PIX), PIX), :]
        on_left = lax.broadcasted_iota(jnp.int32, (PIX, LANES), 1) < border

        def field(n):
            return jnp.where(on_left, left_pix[:, n : n + 1], right_pix[:, n : n + 1])

        inv_square = field(3)
        squares = None
        grad_trans = None
        along = None
        for c in range(3):
            layer = ahead * color[c]
            residual = split_dot(layer, same) + whole - field(c)
            slope = residual * inv_square
            squares = residual * residual if c == 0 else squares + residual * residual
            grad_trans = slope if c == 0 else grad_trans + slope
            along = slope * layer if c == 0 else along + slope * layer
            color[c] = ahead * slope
        loss = 0.5 * squares * inv_square + field(4)
        for h in range(2):
            turned_loss = loss[h * LANES : (h + 1) * LANES].T

            @pl.when(has_first)
            def _():
                loss_ref[pl.ds(2 * t + h, 1), :] = turned_loss[:1]

            @pl.when(has_last)
            def _():
                loss_ref[pl.ds(2 * t + 2 + h, 1), :] = turned_loss[LANES - 1 :]

        follow = split_dot(along, to_right) + grad_trans * whole
        carry[...] = follow / through

        sums[...] = jnp.zeros_like(sums)

        def pull(step, unused):
            behind = [None] * (2 * ROWS)
            slope = [[None] * 3 for _ in range(2 * ROWS)]
            for n in range(2 * ROWS):
                at = pl.ds(pl.multiple_of(step * (ROWS * 16) + 8 * n, 8), 8)
                behind[n] = carry[at, :]
                slope[n] = [color[c, at, :] for c in range(3)]
            for k in range(SPLATS - 1, -1, -1):
                shade = [rows[k * 9 + 6 + c] for c in range(3)]
                acc = [None] * 9

                def add(n, value):
                    acc[n] = value if acc[n] is None else acc[n] + value

                for r in range(ROWS):
                    down = unit_y(k, r, step)
                    for h in range(2):
                        n = 2 * r + h
                        alpha = alphas[step, k, n]
                        weight = weights[step, k, n]
                        gain = slope[n][0] * shade[0] + slope[n][1] * shade[1] + slope[n][2] * shade[2]
                        change = gain - behind[n]
                        behind[n] = behind[n] + alpha * change
                        pulled = weight * change
                        leaned = pulled * down
                        add(3 * h, pulled)
                        add(3 * h + 1, leaned)
                        add(3 * h + 2, leaned * down)
                        for c in range(3):
                            add(6 + c, weight * slope[n][c])
                for n in range(9):
                    sums[k * 9 + n] = sums[k * 9 + n] + acc[n]
            return 0

        lax.fori_loop(0, STEPS, pull, 0)

        plain_sums = [None] * 9
        for k in range(SPLATS):
            chosen = ranks == float(k)
            left, right = [[sums[k * 9 + 3 * h + n] for n in range(3)] for h in range(2)]
            u0, u1 = across[k, 0, 0], across[k, 1, 0]
            m0, m1 = left[0] * u0, right[0] * u1
            moments = [
                left[0] + right[0],
                m0 + m1,
                left[1] + right[1],
                m0 * u0 + m1 * u1,
                left[1] * u0 + right[1] * u1,
                left[2] + right[2],
            ] + [sums[k * 9 + 6 + c] for c in range(3)]
            for n, value in enumerate(moments):
                row = jnp.broadcast_to(jnp.sum(value, axis=0, keepdims=True), (8, LANES))
                plain_sums[n] = (
                    jnp.where(chosen, row, 0.0) if k == 0 else jnp.where(chosen, row, plain_sums[n])
                )
        s0, su, sv, suu, suv, svv = plain_sums[:6]
        inv_scale = 1.0 / scale
        su, sv = su * inv_scale, sv * inv_scale
        inv_both = inv_scale * inv_scale
        suu, suv, svv = suu * inv_both, suv * inv_both, svv * inv_both
        result = [
            inv_det * inv_x * (su - rho * sv),
            inv_det * inv_y * (sv - rho * su),
            inv_det * (suu - rho * suv),
            inv_det * (svv - rho * suv),
            inv_det
            * (suv - rho * inv_det * (suu - 2.0 * rho * suv + svv))
            * (0.9 * (1.0 - curl * curl)),
            s0 * (1.0 - odds),
        ] + [plain_sums[6 + c] * tint[c] * (1.0 - tint[c]) for c in range(3)]
        for here, at in ((has_first, t), (has_last, t + 1)):

            @pl.when(here)
            def _():
                place = places[at]
                for p in range(9):
                    value = jnp.take_along_axis(result[p], jnp.maximum(place, 0), axis=1)
                    grads[pl.ds(pl.multiple_of(32 * p + 8 * at, 8), 8), :] = jnp.where(
                        place >= 0, value, 0.0
                    )

    grads[pl.ds(288, 96), :] = jnp.zeros((96, LANES), F32)
    lax.fori_loop(0, 4, block, 0)
    for b in range(3):
        out_ref[pl.ds(b, LANES, stride=3), :] = grads[pl.ds(b * LANES, LANES), :].T


def order_matrix(regions):
    levels = regions.bit_length() - 1
    turns = np.zeros((regions - 1, regions), np.float32)
    for r in range(regions):
        for d in range(levels):
            bit = (r >> (levels - 1 - d)) & 1
            turns[2**d - 1 + (r >> (levels - d)), r] = (1 - 2 * bit) * 2 ** (levels - 1 - d)
    return turns


def vmem(*shape, dtype=F32):
    return pltpu.VMEM(shape, dtype)


def shards(gaussians, depth, coverage, flips, features, w_first, b_first, w_second, target):
    regions = lax.axis_size("region")
    my_index = lax.axis_index("region")
    limit = pltpu.CompilerParams(vmem_limit_bytes=32 * 1024 * 1024)

    whole = pltpu.CompilerParams(vmem_limit_bytes=60 * 1024 * 1024)

    def exchange(rows):
        moved = lax.all_to_all(rows.reshape(regions, 1, WIDTH), "region", 0, 0, tiled=True)
        return moved.reshape(rows.shape)

    message = pl.pallas_call(
        pack_kernel,
        out_shape=jax.ShapeDtypeStruct((3 * regions, LANES), F32),
        scratch_shapes=[vmem(512, LANES), vmem(LANES, LANES)],
        compiler_params=whole,
        name="pack",
    )(gaussians.reshape(9, 32, LANES), depth[0].T, coverage)
    received = exchange(message)

    pix = pl.pallas_call(
        pixel_kernel,
        grid=(4,),
        in_specs=[
            pl.BlockSpec((PIX, 384), lambda i: (i, 0)),
            pl.BlockSpec((384, 384), lambda i: (0, 0)),
            pl.BlockSpec((1, 384), lambda i: (0, 0)),
            pl.BlockSpec((1, 384), lambda i: (0, 0)),
            pl.BlockSpec((3, PIX), lambda i: (0, i)),
        ],
        out_specs=pl.BlockSpec((PIX, LANES), lambda i: (i, 0)),
        out_shape=jax.ShapeDtypeStruct((4 * PIX, LANES), F32),
        compiler_params=limit,
        cost_estimate=pl.CostEstimate(
            flops=2 * 1024 * 384 * 512, bytes_accessed=2_000_000, transcendentals=1024 * 384
        ),
        name="pixels",
    )(features, w_first, b_first[None], w_second[None], target)

    my_flips = lax.dynamic_slice_in_dim(flips, my_index * 4, 4, 0).astype(F32)
    turned = jnp.dot(my_flips, jnp.asarray(order_matrix(regions)), precision=lax.Precision.HIGHEST)
    rank = jnp.arange(regions, dtype=F32)[None] + turned
    before = (rank[:, :, None] < rank[:, None, :]).astype(BF16)
    behind = (rank[:, :, None] > rank[:, None, :]).astype(BF16)

    loss, returned = pl.pallas_call(
        splat_kernel,
        out_shape=(
            jax.ShapeDtypeStruct((8, LANES), F32),
            jax.ShapeDtypeStruct((3 * regions, LANES), F32),
        ),
        scratch_shapes=[
            vmem(WIDTH, LANES),
            vmem(4, 8, LANES, dtype=jnp.int32),
            vmem(4, 8, LANES, dtype=jnp.int32),
            vmem(72, 8, LANES),
            vmem(SPLATS, 2, 3, 8, LANES),
            vmem(STEPS, SPLATS, 2 * ROWS, 8, LANES),
            vmem(STEPS, SPLATS, 2 * ROWS, 8, LANES),
            vmem(PIX, LANES),
            vmem(3, PIX, LANES),
            vmem(PIX, LANES),
            vmem(72, 8, LANES),
            vmem(WIDTH, LANES),
        ],
        compiler_params=limit,
        name="splats",
    )(received, pix, before, behind)

    back = exchange(returned)
    splat_grads = pl.pallas_call(
        unpack_kernel,
        out_shape=jax.ShapeDtypeStruct((9, 32, LANES), F32),
        compiler_params=limit,
        name="unpack",
    )(back)
    return loss.reshape(4 * PIX), splat_grads.reshape(1, 9, 32 * LANES)


def solution(mesh):
    placed = (
        P("region", None, None),
        P("region", None, None),
        P("region", None),
        P(),
        P("region", None),
        P(),
        P(),
        P(),
        P(None, "region"),
    )
    return jax.shard_map(
        shards,
        mesh=mesh,
        in_specs=placed,
        out_specs=(P("region"), P("region", None, None)),
        check_vma=False,
    )
```

```python
import math

import jax
import jax.numpy as jnp
import numpy as np
from jax import lax
from jax.experimental import pallas as pl
from jax.experimental.pallas import tpu as pltpu
from jax.sharding import PartitionSpec as P

TSIDE = 16
PIX = TSIDE * TSIDE
SPLATS = 8
LANES = 128
WIDTH = 384
HALF_LOG2E = 0.5 * math.log2(math.e)
F32 = jnp.float32
BF16 = jnp.bfloat16


def cut_columns(source, shift):
    return pltpu.roll(source, shift, 1) if shift else source


def pack_kernel(gauss_ref, depth_ref, cover_ref, out_ref, turned, strided):
    group = lax.broadcasted_iota(jnp.int32, (32, LANES), 1) // 32
    for part in range(3):
        for d in range(4):
            block = None
            for a in range(min(4, 9 - 4 * part)):
                moved = cut_columns(gauss_ref[4 * part + a], 32 * ((a - d) % 4))
                block = moved if block is None else jnp.where(group == a, moved, block)
            if part < 2:
                out_ref[pl.ds(3 * d + part, 32, stride=12), :] = block
            else:
                strided[pl.ds(d, 32, stride=4), :] = block
    ranks = depth_ref[...].astype(F32)
    covered = cover_ref[...].astype(F32)
    filler = jnp.zeros((LANES - 16, 512), F32)
    row = lax.broadcasted_iota(jnp.int32, (8, 512), 0)
    covered = jnp.where(row == 0, jnp.broadcast_to(covered, (8, 512)), 0.0)
    stacked = jnp.concatenate([ranks, covered, filler], 0)
    for b in range(4):
        turned[pl.ds(b * LANES, LANES), :] = stacked[:, b * LANES : (b + 1) * LANES].T
    tail = None
    for t in range(4):
        moved = pltpu.roll(turned[pl.ds(t, LANES, stride=4), :], 32 + 16 * t, 1)
        tail = moved if tail is None else tail + moved
    lane = lax.broadcasted_iota(jnp.int32, (LANES, LANES), 1)
    out_ref[pl.ds(2, LANES, stride=3), :] = jnp.where(lane < 32, strided[...], tail)


def unpack_kernel(msg_ref, out_ref):
    group = lax.broadcasted_iota(jnp.int32, (32, LANES), 1) // 32
    for p in range(9):
        a, part = p % 4, p // 4
        block = None
        for d in range(4):
            moved = cut_columns(msg_ref[pl.ds(3 * d + part, 32, stride=12), :], 32 * ((d - a) % 4))
            block = moved if block is None else jnp.where(group == d, moved, block)
        out_ref[p] = block


def pixel_kernel(
    w_first_hbm, b_first_hbm, w_second_hbm, feat_hbm, target_hbm, flips_hbm, turns_hbm,
    pix_ref, before_ref, behind_ref,
    w_first_ref, b_first_ref, w_second_ref, feat_ref, target_ref, flips_ref, turns_ref, arrived,
):
    me = lax.axis_index("region")
    first_row = pl.multiple_of(8 * (me // 2), 8)
    pairs = [
        (w_first_hbm, w_first_ref),
        (b_first_hbm, b_first_ref),
        (w_second_hbm, w_second_ref),
        (target_hbm, target_ref),
        (flips_hbm.at[pl.ds(first_row, 8), :], flips_ref),
        (turns_hbm, turns_ref),
    ] + [(feat_hbm.at[pl.ds(t * PIX, PIX), :], feat_ref.at[pl.ds(t * PIX, PIX), :]) for t in range(4)]
    fetches = [
        pltpu.make_async_copy(source, landing, arrived.at[n])
        for n, (source, landing) in enumerate(pairs)
    ]
    for fetch in fetches:
        fetch.start()
    for fetch in fetches[:6]:
        fetch.wait()
    rows = jnp.broadcast_to(w_second_ref[...][None, :], (LANES, w_second_ref.shape[0]))
    bias = b_first_ref[...][None, :]
    lane = lax.broadcasted_iota(jnp.int32, (PIX, LANES), 1)
    filler = jnp.zeros((LANES - 3, PIX), F32)
    for t in range(4):
        fetches[6 + t].wait()
        at = pl.ds(t * PIX, PIX)
        pre = jnp.dot(feat_ref[at, :], w_first_ref[...], preferred_element_type=F32) + bias
        hidden = jax.nn.gelu(pre).astype(BF16)
        score = lax.dot_general(
            hidden, rows, (((1,), (1,)), ((), ())), preferred_element_type=F32
        )
        spread = 0.5 + (jnp.maximum(score, 0.0) + jnp.log1p(jnp.exp(-jnp.abs(score))))
        wanted = jnp.concatenate([target_ref[:, t * PIX : (t + 1) * PIX], filler], 0).T
        pix_ref[at, :] = jnp.where(
            lane == 3, 1.0 / (spread * spread), jnp.where(lane == 4, jnp.log(spread), wanted)
        )
    turned = jnp.dot(
        flips_ref[...].astype(F32).astype(BF16), turns_ref[...], preferred_element_type=F32
    )
    ranks = jnp.where(me % 2 == 0, turned[:4], turned[4:])
    ranks = ranks + lax.broadcasted_iota(jnp.int32, (4, LANES), 1).astype(F32)
    for t in range(4):
        across = jnp.broadcast_to(ranks[t : t + 1], (LANES, LANES))
        down = across.T
        before_ref[t] = jnp.where(down < across, 1.0, 0.0).astype(BF16)
        behind_ref[t] = jnp.where(down > across, 1.0, 0.0).astype(BF16)


def split_dot(value, matrix):
    high = value.astype(BF16)
    low = (value - high.astype(F32)).astype(BF16)
    return jnp.dot(high, matrix, preferred_element_type=F32) + jnp.dot(
        low, matrix, preferred_element_type=F32
    )


ROWS = 4
STEPS = TSIDE // ROWS


def splat_kernel(
    msg_ref, pix_ref, before_ref, behind_ref, loss_ref, out_ref,
    turned, places, sources, rows, across, alphas, weights, clear, color, carry, sums, grads,
):
    last_part = msg_ref[pl.ds(2, LANES, stride=3), :]
    turned[pl.ds(2 * LANES, LANES), :] = last_part.T
    for b in range(2):
        turned[pl.ds(b * LANES, LANES), :] = msg_ref[pl.ds(b, LANES, stride=3), :].T
    sub = lax.broadcasted_iota(jnp.int32, (8, LANES), 0).astype(F32)
    lane = lax.broadcasted_iota(jnp.int32, (LANES, LANES), 1)
    line = lax.broadcasted_iota(jnp.int32, (LANES, LANES), 0)
    loss_ref[...] = jnp.zeros_like(loss_ref)
    grads[...] = jnp.zeros_like(grads)

    counts = []
    for t in range(4):
        kept = jnp.where(lane[:8] == 0, 1.0, turned[pl.ds(288 + 16 * t + 8, 1), :])
        kept_down = jnp.where(line == 0, 1.0, last_part[:, 32 + 16 * t + 8 : 32 + 16 * t + 9])
        counts.append(jnp.sum(kept[:1]).astype(jnp.int32))
        if t % 2 == 0:
            ahead_of, ahead_down = before_ref[t], behind_ref[t]
        else:
            ahead_of, ahead_down = behind_ref[t], before_ref[t]
        spot = jnp.dot(kept.astype(BF16), ahead_of, preferred_element_type=F32)
        spot_down = jnp.dot(ahead_down, kept_down.astype(BF16), preferred_element_type=F32)
        if t % 2 == 1:
            spot, spot_down = (LANES - 1.0) - spot, (LANES - 1.0) - spot_down
        places[t] = jnp.where(kept > 0.0, spot, -1.0).astype(jnp.int32)
        hit = jnp.logical_and(kept_down > 0.0, spot_down == lane.astype(F32))
        source = jnp.sum(jnp.where(hit, line.astype(F32), 0.0), axis=0, keepdims=True)
        sources[t] = jnp.broadcast_to(source, (8, LANES)).astype(jnp.int32)

    fits = [counts[2 * s] + counts[2 * s + 1] <= LANES for s in range(2)]

    def unit_y(s, k, step, r):
        at = (step * ROWS + r).astype(F32) + 0.5
        return (at - rows[s, k * 9 + 1]) * rows[s, k * 9 + 3]

    def render(step, unused):
        for s in range(2):
            trans = [[None] * 2 for _ in range(ROWS)]
            total = [[[None] * 3 for _ in range(2)] for _ in range(ROWS)]
            for k in range(SPLATS):
                shade = [rows[s, k * 9 + 6 + c] for c in range(3)]
                for r in range(ROWS):
                    down = unit_y(s, k, step, r)
                    for h in range(2):
                        power = down * (across[s, k, h, 1] - down) - across[s, k, h, 2]
                        alpha = jnp.exp2(power)
                        weight = alpha if k == 0 else trans[r][h] * alpha
                        trans[r][h] = 1.0 - alpha if k == 0 else trans[r][h] - weight
                        alphas[s, step, k, 2 * r + h] = alpha
                        weights[s, step, k, 2 * r + h] = weight
                        for c in range(3):
                            term = weight * shade[c]
                            total[r][h][c] = term if k == 0 else total[r][h][c] + term
            for r in range(ROWS):
                for h in range(2):
                    at = pl.ds(pl.multiple_of((step * ROWS + r) * 16 + 8 * h, 8), 8)
                    clear[s, at, :] = trans[r][h]
                    for c in range(3):
                        color[s, c, at, :] = total[r][h][c]
        return 0

    def pull(step, unused):
        for s in range(2):
            behind = [None] * (2 * ROWS)
            slope = [[None] * 3 for _ in range(2 * ROWS)]
            for n in range(2 * ROWS):
                at = pl.ds(pl.multiple_of(step * (ROWS * 16) + 8 * n, 8), 8)
                behind[n] = carry[s, at, :]
                slope[n] = [color[s, c, at, :] for c in range(3)]
            for k in range(SPLATS - 1, -1, -1):
                shade = [rows[s, k * 9 + 6 + c] for c in range(3)]
                acc = [None] * 9

                def add(n, value):
                    acc[n] = value if acc[n] is None else acc[n] + value

                for r in range(ROWS):
                    down = unit_y(s, k, step, r)
                    for h in range(2):
                        n = 2 * r + h
                        alpha = alphas[s, step, k, n]
                        weight = weights[s, step, k, n]
                        gain = slope[n][0] * shade[0] + slope[n][1] * shade[1] + slope[n][2] * shade[2]
                        change = gain - behind[n]
                        behind[n] = behind[n] + alpha * change
                        pulled = weight * change
                        leaned = pulled * down
                        add(3 * h, pulled)
                        add(3 * h + 1, leaned)
                        add(3 * h + 2, leaned * down)
                        for c in range(3):
                            add(6 + c, weight * slope[n][c])
                for n in range(9):
                    sums[s, k * 9 + n] = sums[s, k * 9 + n] + acc[n]
        return 0

    def constants(s, has_first, has_last):
        t = 2 * s
        flat = lane[:8]
        in_first = flat < jnp.where(has_first, counts[t], 0)
        in_last = flat >= jnp.where(has_last, LANES - counts[t + 1], LANES)
        first_source, last_source = sources[t], sources[t + 1]

        def pick(at, step, empty=0.0):
            left = jnp.take_along_axis(turned[pl.ds(at, 8), :], first_source, axis=1)
            right = jnp.take_along_axis(turned[pl.ds(at + step, 8), :], last_source, axis=1)
            return jnp.where(in_first, left, jnp.where(in_last, right, empty))

        raw = [pick(32 * p + 8 * t, 8) for p in range(9)]
        ranks = pick(288 + 16 * t, 16, sub)
        covered = pick(288 + 16 * t + 8, 16)[:1]
        inv_x = jnp.exp(-raw[2])
        inv_y = jnp.exp(-raw[3])
        curl = jnp.tanh(raw[4])
        rho = 0.9 * curl
        inv_det = 1.0 / (1.0 - rho * rho)
        scale = jnp.sqrt(HALF_LOG2E * inv_det)
        odds = jax.nn.sigmoid(raw[5])
        tint = [jax.nn.sigmoid(raw[6 + c]) for c in range(3)]
        opacity = 0.99 * odds * covered
        faint = jnp.where(opacity > 0.0, jnp.log2(jnp.maximum(opacity, 1.1754944e-38)), -1e30)
        plain = [raw[0], raw[1], inv_x * scale, inv_y * scale, 2.0 * rho, faint] + tint
        return ranks, inv_x, inv_y, curl, rho, inv_det, scale, odds, tint, plain

    def prepare(s, ranks, plain):
        for k in range(SPLATS):
            chosen = ranks == float(k)
            for n, value in enumerate(plain):
                row = jnp.sum(jnp.where(chosen, value, 0.0), axis=0, keepdims=True)
                rows[s, k * 9 + n] = jnp.broadcast_to(row, (8, LANES))
            for h in range(2):
                unit = (sub + (0.5 + 8.0 * h) - rows[s, k * 9]) * rows[s, k * 9 + 2]
                across[s, k, h, 0] = unit
                across[s, k, h, 1] = unit * rows[s, k * 9 + 4]
                across[s, k, h, 2] = unit * unit - rows[s, k * 9 + 5]

    on_lane = lax.broadcasted_iota(jnp.int32, (PIX, LANES), 1)

    def composite(flags):
        borders, logs, sames, rights = [], [], [], []
        for s, (has_first, has_last) in enumerate(flags):
            border = jnp.where(has_first, jnp.where(has_last, counts[2 * s], LANES), 0)
            same = (lane < border) == (line < border)
            left = jnp.where(jnp.logical_and(same, line < lane), 1.0, 0.0).astype(BF16)
            rights.append(jnp.where(jnp.logical_and(same, line > lane), 1.0, 0.0).astype(BF16))
            sames.append(jnp.where(same, 1.0, 0.0).astype(BF16))
            borders.append(border)
            logs.append(split_dot(jnp.log(clear[s]), jnp.concatenate([left, sames[s]], 1)))
        losses = []
        alongs, grad_transes = [], []
        for s in range(2):
            ahead = jnp.exp(logs[s][:, :LANES])
            whole = jnp.exp(logs[s][:, LANES:])
            left_pix = pix_ref[pl.ds(2 * s * PIX, PIX), :]
            right_pix = pix_ref[pl.ds((2 * s + 1) * PIX, PIX), :]
            on_left = on_lane < borders[s]

            def field(n):
                return jnp.where(on_left, left_pix[:, n : n + 1], right_pix[:, n : n + 1])

            inv_square = field(3)
            squares = None
            grad_trans = None
            along = None
            for c in range(3):
                layer = ahead * color[s, c]
                residual = split_dot(layer, sames[s]) + whole - field(c)
                slope = residual * inv_square
                squares = residual * residual if c == 0 else squares + residual * residual
                grad_trans = slope if c == 0 else grad_trans + slope
                along = slope * layer if c == 0 else along + slope * layer
                color[s, c] = ahead * slope
            losses.append(0.5 * squares * inv_square + field(4))
            alongs.append(along)
            grad_transes.append(grad_trans * whole)
        for s, (has_first, has_last) in enumerate(flags):
            follow = split_dot(alongs[s], rights[s]) + grad_transes[s]
            carry[s] = follow / clear[s]
        for s, (has_first, has_last) in enumerate(flags):
            for h in range(2):
                shown = losses[s][h * LANES : (h + 1) * LANES].T
                for here, row, value in (
                    (has_first, 4 * s + h, shown[:1]),
                    (has_last, 4 * s + 2 + h, shown[LANES - 1 :]),
                ):
                    loss_ref[row : row + 1, :] = jnp.where(here, value, loss_ref[row : row + 1, :])

    def finish(s, flag, ranks, inv_x, inv_y, curl, rho, inv_det, scale, odds, tint):
        plain_sums = [None] * 9
        for k in range(SPLATS):
            chosen = ranks == float(k)
            left, right = [[sums[s, k * 9 + 3 * h + n] for n in range(3)] for h in range(2)]
            u0, u1 = across[s, k, 0, 0], across[s, k, 1, 0]
            m0, m1 = left[0] * u0, right[0] * u1
            moments = [
                left[0] + right[0],
                m0 + m1,
                left[1] + right[1],
                m0 * u0 + m1 * u1,
                left[1] * u0 + right[1] * u1,
                left[2] + right[2],
            ] + [sums[s, k * 9 + 6 + c] for c in range(3)]
            for n, value in enumerate(moments):
                row = jnp.broadcast_to(jnp.sum(value, axis=0, keepdims=True), (8, LANES))
                plain_sums[n] = (
                    jnp.where(chosen, row, 0.0) if k == 0 else jnp.where(chosen, row, plain_sums[n])
                )
        s0, su, sv, suu, suv, svv = plain_sums[:6]
        inv_scale = 1.0 / scale
        su, sv = su * inv_scale, sv * inv_scale
        inv_both = inv_scale * inv_scale
        suu, suv, svv = suu * inv_both, suv * inv_both, svv * inv_both
        result = [
            inv_det * inv_x * (su - rho * sv),
            inv_det * inv_y * (sv - rho * su),
            inv_det * (suu - rho * suv),
            inv_det * (svv - rho * suv),
            inv_det
            * (suv - rho * inv_det * (suu - 2.0 * rho * suv + svv))
            * (0.9 * (1.0 - curl * curl)),
            s0 * (1.0 - odds),
        ] + [plain_sums[6 + c] * tint[c] * (1.0 - tint[c]) for c in range(3)]
        for here, t in zip(flag, (2 * s, 2 * s + 1)):
            place = places[t]
            taken = jnp.logical_and(place >= 0, here)
            place = jnp.maximum(place, 0)
            for p in range(9):
                at = pl.ds(32 * p + 8 * t, 8)
                value = jnp.take_along_axis(result[p], place, axis=1)
                grads[at, :] = jnp.where(taken, value, grads[at, :])

    def both_blocks(turn, unused):
        opening = turn == 0
        flags = [(opening, jnp.logical_xor(fits[s], turn == 1)) for s in range(2)]
        held = [constants(s, *flags[s]) for s in range(2)]
        for s in range(2):
            prepare(s, held[s][0], held[s][-1])
        lax.fori_loop(0, STEPS, render, 0)
        composite(flags)
        sums[...] = jnp.zeros_like(sums)
        lax.fori_loop(0, STEPS, pull, 0)
        for s in range(2):
            finish(s, flags[s], *held[s][:-1])
        return 0

    turns = jnp.where(jnp.logical_and(fits[0], fits[1]), 1, 2)
    lax.fori_loop(0, turns, both_blocks, 0)
    for b in range(3):
        out_ref[pl.ds(b, LANES, stride=3), :] = grads[pl.ds(b * LANES, LANES), :].T


def order_matrix(regions):
    levels = regions.bit_length() - 1
    turns = np.zeros((regions - 1, regions), np.float32)
    for r in range(regions):
        for d in range(levels):
            bit = (r >> (levels - 1 - d)) & 1
            turns[2**d - 1 + (r >> (levels - d)), r] = (1 - 2 * bit) * 2 ** (levels - 1 - d)
    return turns


def vmem(*shape, dtype=F32):
    return pltpu.VMEM(shape, dtype)


def shards(gaussians, depth, coverage, flips, features, w_first, b_first, w_second, target):
    regions = lax.axis_size("region")
    my_index = lax.axis_index("region")
    limit = pltpu.CompilerParams(vmem_limit_bytes=32 * 1024 * 1024)

    whole = pltpu.CompilerParams(vmem_limit_bytes=60 * 1024 * 1024)

    def exchange(rows):
        moved = lax.all_to_all(rows.reshape(regions, 1, WIDTH), "region", 0, 0, tiled=True)
        return moved.reshape(rows.shape)

    message = pl.pallas_call(
        pack_kernel,
        out_shape=jax.ShapeDtypeStruct((3 * regions, LANES), F32),
        scratch_shapes=[vmem(512, LANES), vmem(LANES, LANES)],
        compiler_params=whole,
        name="pack",
    )(gaussians.reshape(9, 32, LANES), depth[0].T, coverage)
    received = exchange(message)

    order = jax.ShapeDtypeStruct((4, LANES, LANES), BF16)
    operands = (
        w_first, b_first, w_second, features, target, flips, jnp.asarray(order_matrix(regions), BF16)
    )
    landings = [pltpu.VMEM(x.shape, x.dtype) for x in operands]
    landings[5] = pltpu.VMEM((8, regions - 1), jnp.int32)
    pix, before, behind = pl.pallas_call(
        pixel_kernel,
        in_specs=[pl.BlockSpec(memory_space=pltpu.HBM)] * 7,
        out_shape=(jax.ShapeDtypeStruct((4 * PIX, LANES), F32), order, order),
        scratch_shapes=landings + [pltpu.SemaphoreType.DMA((10,))],
        compiler_params=limit,
        cost_estimate=pl.CostEstimate(
            flops=2 * 1024 * 384 * 512, bytes_accessed=2_000_000, transcendentals=1024 * 384
        ),
        name="pixels",
    )(*operands)

    loss, returned = pl.pallas_call(
        splat_kernel,
        out_shape=(
            jax.ShapeDtypeStruct((8, LANES), F32),
            jax.ShapeDtypeStruct((3 * regions, LANES), F32),
        ),
        scratch_shapes=[
            vmem(WIDTH, LANES),
            vmem(4, 8, LANES, dtype=jnp.int32),
            vmem(4, 8, LANES, dtype=jnp.int32),
            vmem(2, 72, 8, LANES),
            vmem(2, SPLATS, 2, 3, 8, LANES),
            vmem(2, STEPS, SPLATS, 2 * ROWS, 8, LANES),
            vmem(2, STEPS, SPLATS, 2 * ROWS, 8, LANES),
            vmem(2, PIX, LANES),
            vmem(2, 3, PIX, LANES),
            vmem(2, PIX, LANES),
            vmem(2, 72, 8, LANES),
            vmem(WIDTH, LANES),
        ],
        compiler_params=limit,
        name="splats",
    )(received, pix, before, behind)

    back = exchange(returned)
    splat_grads = pl.pallas_call(
        unpack_kernel,
        out_shape=jax.ShapeDtypeStruct((9, 32, LANES), F32),
        compiler_params=limit,
        name="unpack",
    )(back)
    return loss.reshape(4 * PIX), splat_grads.reshape(1, 9, 32 * LANES)


def solution(mesh):
    placed = (
        P("region", None, None),
        P("region", None, None),
        P("region", None),
        P(),
        P("region", None),
        P(),
        P(),
        P(),
        P(None, "region"),
    )
    return jax.shard_map(
        shards,
        mesh=mesh,
        in_specs=placed,
        out_specs=(P("region"), P("region", None, None)),
        check_vma=False,
    )
```

```python
import math

import jax
import jax.numpy as jnp
import numpy as np
from jax import lax
from jax.experimental import pallas as pl
from jax.experimental.pallas import tpu as pltpu
from jax.sharding import PartitionSpec as P

TSIDE = 16
PIX = TSIDE * TSIDE
SPLATS = 8
LANES = 128
WIDTH = 384
HALF_LOG2E = 0.5 * math.log2(math.e)
F32 = jnp.float32
BF16 = jnp.bfloat16


def cut_columns(source, shift):
    return pltpu.roll(source, shift, 1) if shift else source


def pack_kernel(gauss_ref, depth_ref, cover_ref, out_ref, turned, strided):
    group = lax.broadcasted_iota(jnp.int32, (32, LANES), 1) // 32
    for part in range(3):
        for d in range(4):
            block = None
            for a in range(min(4, 9 - 4 * part)):
                moved = cut_columns(gauss_ref[4 * part + a], 32 * ((a - d) % 4))
                block = moved if block is None else jnp.where(group == a, moved, block)
            if part < 2:
                out_ref[pl.ds(3 * d + part, 32, stride=12), :] = block
            else:
                strided[pl.ds(d, 32, stride=4), :] = block
    ranks = depth_ref[...].astype(F32)
    covered = cover_ref[...].astype(F32)
    filler = jnp.zeros((LANES - 16, 512), F32)
    row = lax.broadcasted_iota(jnp.int32, (8, 512), 0)
    covered = jnp.where(row == 0, jnp.broadcast_to(covered, (8, 512)), 0.0)
    stacked = jnp.concatenate([ranks, covered, filler], 0)
    for b in range(4):
        turned[pl.ds(b * LANES, LANES), :] = stacked[:, b * LANES : (b + 1) * LANES].T
    tail = None
    for t in range(4):
        moved = pltpu.roll(turned[pl.ds(t, LANES, stride=4), :], 32 + 16 * t, 1)
        tail = moved if tail is None else tail + moved
    lane = lax.broadcasted_iota(jnp.int32, (LANES, LANES), 1)
    out_ref[pl.ds(2, LANES, stride=3), :] = jnp.where(lane < 32, strided[...], tail)


def unpack_kernel(msg_ref, out_ref):
    group = lax.broadcasted_iota(jnp.int32, (32, LANES), 1) // 32
    for p in range(9):
        a, part = p % 4, p // 4
        block = None
        for d in range(4):
            moved = cut_columns(msg_ref[pl.ds(3 * d + part, 32, stride=12), :], 32 * ((d - a) % 4))
            block = moved if block is None else jnp.where(group == d, moved, block)
        out_ref[p] = block


def pixel_kernel(
    feat_ref, w_first_ref, b_first_ref, w_second_ref, target_ref, flips_hbm, turns_ref,
    pix_ref, before_ref, behind_ref, flipped, arrived,
):
    me = lax.axis_index("region")
    first_row = pl.multiple_of(8 * (me // 2), 8)
    fetch = pltpu.make_async_copy(flips_hbm.at[pl.ds(first_row, 8), :], flipped, arrived)
    fetch.start()
    rows = jnp.broadcast_to(w_second_ref[...][None, :], (16, w_second_ref.shape[0]))
    filler = jnp.zeros((LANES - 8, PIX), F32)
    row = lax.broadcasted_iota(jnp.int32, (8, PIX), 0)
    bias = b_first_ref[...][None, :]
    for t in range(4):
        at = pl.ds(t * PIX, PIX)
        pre = jnp.dot(feat_ref[at, :], w_first_ref[...], preferred_element_type=F32) + bias
        hidden = jax.nn.gelu(pre).astype(BF16)
        score = lax.dot_general(
            rows, hidden, (((1,), (1,)), ((), ())), preferred_element_type=F32
        )[:8]
        spread = 0.5 + (jnp.maximum(score, 0.0) + jnp.log1p(jnp.exp(-jnp.abs(score))))
        rest = jnp.where(row == 3, 1.0 / (spread * spread), jnp.log(spread))
        wanted = target_ref[:, t * PIX : (t + 1) * PIX]
        for c in range(3):
            rest = jnp.where(row == c, wanted[c : c + 1], rest)
        pix_ref[at, :] = jnp.concatenate([rest, filler], 0).T
    fetch.wait()
    turned = jnp.dot(
        flipped[...].astype(F32).astype(BF16), turns_ref[...], preferred_element_type=F32
    )
    ranks = jnp.where(me % 2 == 0, turned[:4], turned[4:])
    ranks = ranks + lax.broadcasted_iota(jnp.int32, (4, LANES), 1).astype(F32)
    for t in range(4):
        across = jnp.broadcast_to(ranks[t : t + 1], (LANES, LANES))
        down = across.T
        before_ref[t] = jnp.where(down < across, 1.0, 0.0).astype(BF16)
        behind_ref[t] = jnp.where(down > across, 1.0, 0.0).astype(BF16)


def split_dot(value, matrix):
    high = value.astype(BF16)
    low = (value - high.astype(F32)).astype(BF16)
    return jnp.dot(high, matrix, preferred_element_type=F32) + jnp.dot(
        low, matrix, preferred_element_type=F32
    )


RENDER_ROWS = 4
PULL_ROWS = 4


def splat_kernel(
    msg_ref, pix_ref, before_ref, behind_ref, loss_hbm, out_ref,
    turned, places, sources, rows, across, alphas, weights, clear, color, carry, sums, grads,
    loss_ref, sent,
):
    last_part = msg_ref[pl.ds(2, LANES, stride=3), :]
    turned[pl.ds(2 * LANES, LANES), :] = last_part.T
    for b in range(2):
        turned[pl.ds(b * LANES, LANES), :] = msg_ref[pl.ds(b, LANES, stride=3), :].T
    sub = lax.broadcasted_iota(jnp.int32, (8, LANES), 0).astype(F32)
    lane = lax.broadcasted_iota(jnp.int32, (LANES, LANES), 1)
    line = lax.broadcasted_iota(jnp.int32, (LANES, LANES), 0)
    loss_ref[...] = jnp.zeros_like(loss_ref)
    grads[...] = jnp.zeros_like(grads)

    counts = []
    for t in range(4):
        kept = jnp.where(lane[:8] == 0, 1.0, turned[pl.ds(288 + 16 * t + 8, 1), :])
        kept_down = jnp.where(line == 0, 1.0, last_part[:, 32 + 16 * t + 8 : 32 + 16 * t + 9])
        counts.append(jnp.sum(kept[:1]).astype(jnp.int32))
        if t % 2 == 0:
            ahead_of, ahead_down = before_ref[t], behind_ref[t]
        else:
            ahead_of, ahead_down = behind_ref[t], before_ref[t]
        spot = jnp.dot(kept.astype(BF16), ahead_of, preferred_element_type=F32)
        spot_down = jnp.dot(ahead_down, kept_down.astype(BF16), preferred_element_type=F32)
        if t % 2 == 1:
            spot, spot_down = (LANES - 1.0) - spot, (LANES - 1.0) - spot_down
        places[t] = jnp.where(kept > 0.0, spot, -1.0).astype(jnp.int32)
        hit = jnp.logical_and(kept_down > 0.0, spot_down == lane.astype(F32))
        source = jnp.sum(jnp.where(hit, line.astype(F32), 0.0), axis=0, keepdims=True)
        sources[t] = jnp.broadcast_to(source, (8, LANES)).astype(jnp.int32)

    fits = [counts[2 * s] + counts[2 * s + 1] <= LANES for s in range(2)]

    turns = jnp.where(jnp.logical_and(fits[0], fits[1]), 1, 2)
    send = pltpu.make_async_copy(loss_ref, loss_hbm, sent)

    def unit_y(s, k, row):
        return (row.astype(F32) + 0.5 - rows[s, k * 9 + 1]) * rows[s, k * 9 + 3]

    def render(step, unused):
        for s in range(2):
            trans = [[None] * 2 for _ in range(RENDER_ROWS)]
            total = [[[None] * 3 for _ in range(2)] for _ in range(RENDER_ROWS)]
            for k in range(SPLATS):
                shade = [rows[s, k * 9 + 6 + c] for c in range(3)]
                for r in range(RENDER_ROWS):
                    down = unit_y(s, k, step * RENDER_ROWS + r)
                    for h in range(2):
                        power = down * (across[s, k, h, 1] - down) - across[s, k, h, 2]
                        alpha = jnp.exp2(power)
                        weight = alpha if k == 0 else trans[r][h] * alpha
                        trans[r][h] = 1.0 - alpha if k == 0 else trans[r][h] - weight
                        alphas[s, k, 2 * (step * RENDER_ROWS + r) + h] = alpha
                        weights[s, k, 2 * (step * RENDER_ROWS + r) + h] = weight
                        for c in range(3):
                            term = weight * shade[c]
                            total[r][h][c] = term if k == 0 else total[r][h][c] + term
            for r in range(RENDER_ROWS):
                for h in range(2):
                    at = pl.ds(pl.multiple_of((step * RENDER_ROWS + r) * 16 + 8 * h, 8), 8)
                    clear[s, at, :] = trans[r][h]
                    for c in range(3):
                        color[s, c, at, :] = total[r][h][c]
        return 0

    def pull(step, unused):
        for s in range(2):
            behind = [None] * (2 * PULL_ROWS)
            slope = [[None] * 3 for _ in range(2 * PULL_ROWS)]
            for n in range(2 * PULL_ROWS):
                at = pl.ds(pl.multiple_of(step * (PULL_ROWS * 16) + 8 * n, 8), 8)
                behind[n] = carry[s, at, :]
                slope[n] = [color[s, c, at, :] for c in range(3)]
            for k in range(SPLATS - 1, -1, -1):
                shade = [rows[s, k * 9 + 6 + c] for c in range(3)]
                acc = [None] * 9

                def add(n, value):
                    acc[n] = value if acc[n] is None else acc[n] + value

                for r in range(PULL_ROWS):
                    down = unit_y(s, k, step * PULL_ROWS + r)
                    for h in range(2):
                        n = 2 * r + h
                        alpha = alphas[s, k, 2 * PULL_ROWS * step + n]
                        weight = weights[s, k, 2 * PULL_ROWS * step + n]
                        gain = slope[n][0] * shade[0] + slope[n][1] * shade[1] + slope[n][2] * shade[2]
                        change = gain - behind[n]
                        behind[n] = behind[n] + alpha * change
                        pulled = weight * change
                        leaned = pulled * down
                        add(3 * h, pulled)
                        add(3 * h + 1, leaned)
                        add(3 * h + 2, leaned * down)
                        for c in range(3):
                            add(6 + c, weight * slope[n][c])
                for n in range(9):
                    sums[s, k * 9 + n] = sums[s, k * 9 + n] + acc[n]
        return 0

    def constants(s, has_first, has_last):
        t = 2 * s
        flat = lane[:8]
        in_first = flat < jnp.where(has_first, counts[t], 0)
        in_last = flat >= jnp.where(has_last, LANES - counts[t + 1], LANES)
        first_source, last_source = sources[t], sources[t + 1]

        def pick(at, step, empty=0.0):
            left = jnp.take_along_axis(turned[pl.ds(at, 8), :], first_source, axis=1)
            right = jnp.take_along_axis(turned[pl.ds(at + step, 8), :], last_source, axis=1)
            return jnp.where(in_first, left, jnp.where(in_last, right, empty))

        raw = [pick(32 * p + 8 * t, 8) for p in range(9)]
        ranks = pick(288 + 16 * t, 16, sub)
        covered = pick(288 + 16 * t + 8, 16)[:1]
        inv_x = jnp.exp(-raw[2])
        inv_y = jnp.exp(-raw[3])
        curl = jnp.tanh(raw[4])
        rho = 0.9 * curl
        inv_det = 1.0 / (1.0 - rho * rho)
        scale = jnp.sqrt(HALF_LOG2E * inv_det)
        odds = jax.nn.sigmoid(raw[5])
        tint = [jax.nn.sigmoid(raw[6 + c]) for c in range(3)]
        opacity = 0.99 * odds * covered
        faint = jnp.where(opacity > 0.0, jnp.log2(jnp.maximum(opacity, 1.1754944e-38)), -1e30)
        plain = [raw[0], raw[1], inv_x * scale, inv_y * scale, 2.0 * rho, faint] + tint
        return ranks, inv_x, inv_y, curl, rho, inv_det, scale, odds, tint, plain

    def prepare(s, ranks, plain):
        for k in range(SPLATS):
            chosen = ranks == float(k)
            for n, value in enumerate(plain):
                row = jnp.sum(jnp.where(chosen, value, 0.0), axis=0, keepdims=True)
                rows[s, k * 9 + n] = jnp.broadcast_to(row, (8, LANES))
            for h in range(2):
                unit = (sub + (0.5 + 8.0 * h) - rows[s, k * 9]) * rows[s, k * 9 + 2]
                across[s, k, h, 0] = unit
                across[s, k, h, 1] = unit * rows[s, k * 9 + 4]
                across[s, k, h, 2] = unit * unit - rows[s, k * 9 + 5]

    on_lane = lax.broadcasted_iota(jnp.int32, (PIX, LANES), 1)

    def composite(flags):
        borders, logs, sames, rights = [], [], [], []
        for s, (has_first, has_last) in enumerate(flags):
            border = jnp.where(has_first, jnp.where(has_last, counts[2 * s], LANES), 0)
            same = (lane < border) == (line < border)
            left = jnp.where(jnp.logical_and(same, line < lane), 1.0, 0.0).astype(BF16)
            rights.append(jnp.where(jnp.logical_and(same, line > lane), 1.0, 0.0).astype(BF16))
            sames.append(jnp.where(same, 1.0, 0.0).astype(BF16))
            borders.append(border)
            logs.append(split_dot(jnp.log(clear[s]), jnp.concatenate([left, sames[s]], 1)))
        losses = []
        alongs, grad_transes = [], []
        for s in range(2):
            ahead = jnp.exp(logs[s][:, :LANES])
            whole = jnp.exp(logs[s][:, LANES:])
            left_pix = pix_ref[pl.ds(2 * s * PIX, PIX), :]
            right_pix = pix_ref[pl.ds((2 * s + 1) * PIX, PIX), :]
            on_left = on_lane < borders[s]

            def field(n):
                return jnp.where(on_left, left_pix[:, n : n + 1], right_pix[:, n : n + 1])

            inv_square = field(3)
            squares = None
            grad_trans = None
            along = None
            for c in range(3):
                layer = ahead * color[s, c]
                residual = split_dot(layer, sames[s]) + whole - field(c)
                slope = residual * inv_square
                squares = residual * residual if c == 0 else squares + residual * residual
                grad_trans = slope if c == 0 else grad_trans + slope
                along = slope * layer if c == 0 else along + slope * layer
                color[s, c] = ahead * slope
            losses.append(0.5 * squares * inv_square + field(4))
            alongs.append(along)
            grad_transes.append(grad_trans * whole)
        for s, (has_first, has_last) in enumerate(flags):
            follow = split_dot(alongs[s], rights[s]) + grad_transes[s]
            carry[s] = follow / clear[s]
        for s, (has_first, has_last) in enumerate(flags):
            for h in range(2):
                shown = losses[s][h * LANES : (h + 1) * LANES].T
                for here, row, value in (
                    (has_first, 4 * s + h, shown[:1]),
                    (has_last, 4 * s + 2 + h, shown[LANES - 1 :]),
                ):
                    loss_ref[row : row + 1, :] = jnp.where(here, value, loss_ref[row : row + 1, :])

    def finish(s, flag, ranks, inv_x, inv_y, curl, rho, inv_det, scale, odds, tint):
        plain_sums = [None] * 9
        for k in range(SPLATS):
            chosen = ranks == float(k)
            left, right = [[sums[s, k * 9 + 3 * h + n] for n in range(3)] for h in range(2)]
            u0, u1 = across[s, k, 0, 0], across[s, k, 1, 0]
            m0, m1 = left[0] * u0, right[0] * u1
            moments = [
                left[0] + right[0],
                m0 + m1,
                left[1] + right[1],
                m0 * u0 + m1 * u1,
                left[1] * u0 + right[1] * u1,
                left[2] + right[2],
            ] + [sums[s, k * 9 + 6 + c] for c in range(3)]
            for n, value in enumerate(moments):
                row = jnp.broadcast_to(jnp.sum(value, axis=0, keepdims=True), (8, LANES))
                plain_sums[n] = (
                    jnp.where(chosen, row, 0.0) if k == 0 else jnp.where(chosen, row, plain_sums[n])
                )
        s0, su, sv, suu, suv, svv = plain_sums[:6]
        inv_scale = 1.0 / scale
        su, sv = su * inv_scale, sv * inv_scale
        inv_both = inv_scale * inv_scale
        suu, suv, svv = suu * inv_both, suv * inv_both, svv * inv_both
        result = [
            inv_det * inv_x * (su - rho * sv),
            inv_det * inv_y * (sv - rho * su),
            inv_det * (suu - rho * suv),
            inv_det * (svv - rho * suv),
            inv_det
            * (suv - rho * inv_det * (suu - 2.0 * rho * suv + svv))
            * (0.9 * (1.0 - curl * curl)),
            s0 * (1.0 - odds),
        ] + [plain_sums[6 + c] * tint[c] * (1.0 - tint[c]) for c in range(3)]
        for here, t in zip(flag, (2 * s, 2 * s + 1)):
            place = places[t]
            taken = jnp.logical_and(place >= 0, here)
            place = jnp.maximum(place, 0)
            for p in range(9):
                at = pl.ds(32 * p + 8 * t, 8)
                value = jnp.take_along_axis(result[p], place, axis=1)
                grads[at, :] = jnp.where(taken, value, grads[at, :])

    def both_blocks(turn, unused):
        opening = turn == 0
        flags = [(opening, jnp.logical_xor(fits[s], turn == 1)) for s in range(2)]
        held = [constants(s, *flags[s]) for s in range(2)]
        for s in range(2):
            prepare(s, held[s][0], held[s][-1])
        lax.fori_loop(0, TSIDE // RENDER_ROWS, render, 0)
        composite(flags)

        @pl.when(turn == turns - 1)
        def _():
            send.start()

        sums[...] = jnp.zeros_like(sums)
        lax.fori_loop(0, TSIDE // PULL_ROWS, pull, 0)
        for s in range(2):
            finish(s, flags[s], *held[s][:-1])
        return 0

    lax.fori_loop(0, turns, both_blocks, 0)
    for b in range(3):
        out_ref[pl.ds(b, LANES, stride=3), :] = grads[pl.ds(b * LANES, LANES), :].T
    send.wait()


def order_matrix(regions):
    levels = regions.bit_length() - 1
    turns = np.zeros((regions - 1, regions), np.float32)
    for r in range(regions):
        for d in range(levels):
            bit = (r >> (levels - 1 - d)) & 1
            turns[2**d - 1 + (r >> (levels - d)), r] = (1 - 2 * bit) * 2 ** (levels - 1 - d)
    return turns


def vmem(*shape, dtype=F32):
    return pltpu.VMEM(shape, dtype)


def shards(gaussians, depth, coverage, flips, features, w_first, b_first, w_second, target):
    regions = lax.axis_size("region")
    my_index = lax.axis_index("region")
    limit = pltpu.CompilerParams(vmem_limit_bytes=32 * 1024 * 1024)

    whole = pltpu.CompilerParams(vmem_limit_bytes=60 * 1024 * 1024)

    def exchange(rows):
        moved = lax.all_to_all(rows.reshape(regions, 1, WIDTH), "region", 0, 0, tiled=True)
        return moved.reshape(rows.shape)

    message = pl.pallas_call(
        pack_kernel,
        out_shape=jax.ShapeDtypeStruct((3 * regions, LANES), F32),
        scratch_shapes=[vmem(512, LANES), vmem(LANES, LANES)],
        compiler_params=whole,
        name="pack",
    )(gaussians.reshape(9, 32, LANES), depth[0].T, coverage)
    received = exchange(message)

    order = jax.ShapeDtypeStruct((4, LANES, LANES), BF16)
    pix, before, behind = pl.pallas_call(
        pixel_kernel,
        in_specs=[pl.BlockSpec(memory_space=pltpu.VMEM)] * 5
        + [pl.BlockSpec(memory_space=pl.ANY), pl.BlockSpec(memory_space=pltpu.VMEM)],
        out_shape=(jax.ShapeDtypeStruct((4 * PIX, LANES), F32), order, order),
        scratch_shapes=[vmem(8, regions - 1, dtype=jnp.int32), pltpu.SemaphoreType.DMA],
        compiler_params=limit,
        cost_estimate=pl.CostEstimate(
            flops=2 * 1024 * 384 * 512, bytes_accessed=2_000_000, transcendentals=1024 * 384
        ),
        name="pixels",
    )(
        features, w_first, b_first, w_second, target, flips,
        jnp.asarray(order_matrix(regions), BF16),
    )

    loss, returned = pl.pallas_call(
        splat_kernel,
        in_specs=[pl.BlockSpec(memory_space=pltpu.VMEM)] * 4,
        out_specs=(pl.BlockSpec(memory_space=pl.ANY), pl.BlockSpec(memory_space=pltpu.VMEM)),
        out_shape=(
            jax.ShapeDtypeStruct((8, LANES), F32),
            jax.ShapeDtypeStruct((3 * regions, LANES), F32),
        ),
        scratch_shapes=[
            vmem(WIDTH, LANES),
            vmem(4, 8, LANES, dtype=jnp.int32),
            vmem(4, 8, LANES, dtype=jnp.int32),
            vmem(2, 72, 8, LANES),
            vmem(2, SPLATS, 2, 3, 8, LANES),
            vmem(2, SPLATS, PIX // 8, 8, LANES),
            vmem(2, SPLATS, PIX // 8, 8, LANES),
            vmem(2, PIX, LANES),
            vmem(2, 3, PIX, LANES),
            vmem(2, PIX, LANES),
            vmem(2, 72, 8, LANES),
            vmem(WIDTH, LANES),
            vmem(8, LANES),
            pltpu.SemaphoreType.DMA,
        ],
        compiler_params=limit,
        name="splats",
    )(received, pix, before, behind)

    back = exchange(returned)
    splat_grads = pl.pallas_call(
        unpack_kernel,
        out_shape=jax.ShapeDtypeStruct((9, 32, LANES), F32),
        compiler_params=limit,
        name="unpack",
    )(back)
    return loss.reshape(4 * PIX), splat_grads.reshape(1, 9, 32 * LANES)


def solution(mesh):
    placed = (
        P("region", None, None),
        P("region", None, None),
        P("region", None),
        P(),
        P("region", None),
        P(),
        P(),
        P(),
        P(None, "region"),
    )
    return jax.shard_map(
        shards,
        mesh=mesh,
        in_specs=placed,
        out_specs=(P("region"), P("region", None, None)),
        check_vma=False,
    )
```

```python
import math

import jax
import jax.numpy as jnp
import numpy as np
from jax import lax
from jax.experimental import pallas as pl
from jax.experimental.pallas import tpu as pltpu
from jax.sharding import PartitionSpec as P

TSIDE = 16
PIX = TSIDE * TSIDE
SPLATS = 8
LANES = 128
WIDTH = 384
HALF_LOG2E = 0.5 * math.log2(math.e)
F32 = jnp.float32
BF16 = jnp.bfloat16


def cut_columns(source, shift):
    return pltpu.roll(source, shift, 1) if shift else source


def pack_kernel(gauss_ref, depth_ref, cover_ref, out_ref, turned, strided):
    group = lax.broadcasted_iota(jnp.int32, (32, LANES), 1) // 32
    for part in range(3):
        for d in range(4):
            block = None
            for a in range(min(4, 9 - 4 * part)):
                moved = cut_columns(gauss_ref[4 * part + a], 32 * ((a - d) % 4))
                block = moved if block is None else jnp.where(group == a, moved, block)
            if part < 2:
                out_ref[pl.ds(3 * d + part, 32, stride=12), :] = block
            else:
                strided[pl.ds(d, 32, stride=4), :] = block
    ranks = depth_ref[...].astype(F32)
    covered = cover_ref[...].astype(F32)
    filler = jnp.zeros((LANES - 16, 512), F32)
    row = lax.broadcasted_iota(jnp.int32, (8, 512), 0)
    covered = jnp.where(row == 0, jnp.broadcast_to(covered, (8, 512)), 0.0)
    stacked = jnp.concatenate([ranks, covered, filler], 0)
    for b in range(4):
        turned[pl.ds(b * LANES, LANES), :] = stacked[:, b * LANES : (b + 1) * LANES].T
    tail = None
    for t in range(4):
        moved = pltpu.roll(turned[pl.ds(t, LANES, stride=4), :], 32 + 16 * t, 1)
        tail = moved if tail is None else tail + moved
    lane = lax.broadcasted_iota(jnp.int32, (LANES, LANES), 1)
    out_ref[pl.ds(2, LANES, stride=3), :] = jnp.where(lane < 32, strided[...], tail)


def unpack_kernel(msg_ref, out_ref):
    group = lax.broadcasted_iota(jnp.int32, (32, LANES), 1) // 32
    for p in range(9):
        a, part = p % 4, p // 4
        block = None
        for d in range(4):
            moved = cut_columns(msg_ref[pl.ds(3 * d + part, 32, stride=12), :], 32 * ((d - a) % 4))
            block = moved if block is None else jnp.where(group == d, moved, block)
        out_ref[p] = block


def pixel_kernel(
    feat_ref, w_first_ref, b_first_ref, w_second_ref, target_ref, flips_hbm, turns_ref,
    pix_ref, before_ref, behind_ref, flipped, arrived,
):
    me = lax.axis_index("region")
    first_row = pl.multiple_of(8 * (me // 2), 8)
    fetch = pltpu.make_async_copy(flips_hbm.at[pl.ds(first_row, 8), :], flipped, arrived)
    fetch.start()
    rows = jnp.broadcast_to(w_second_ref[...][None, :], (16, w_second_ref.shape[0]))
    filler = jnp.zeros((LANES - 8, PIX), F32)
    row = lax.broadcasted_iota(jnp.int32, (8, PIX), 0)
    bias = b_first_ref[...][None, :]
    for t in range(4):
        at = pl.ds(t * PIX, PIX)
        pre = jnp.dot(feat_ref[at, :], w_first_ref[...], preferred_element_type=F32) + bias
        hidden = jax.nn.gelu(pre).astype(BF16)
        score = lax.dot_general(
            rows, hidden, (((1,), (1,)), ((), ())), preferred_element_type=F32
        )[:8]
        spread = 0.5 + (jnp.maximum(score, 0.0) + jnp.log1p(jnp.exp(-jnp.abs(score))))
        rest = jnp.where(row == 3, 1.0 / (spread * spread), jnp.log(spread))
        wanted = target_ref[:, t * PIX : (t + 1) * PIX]
        for c in range(3):
            rest = jnp.where(row == c, wanted[c : c + 1], rest)
        pix_ref[at, :] = jnp.concatenate([rest, filler], 0).T
    fetch.wait()
    turned = jnp.dot(
        flipped[...].astype(F32).astype(BF16), turns_ref[...], preferred_element_type=F32
    )
    ranks = jnp.where(me % 2 == 0, turned[:4], turned[4:])
    ranks = ranks + lax.broadcasted_iota(jnp.int32, (4, LANES), 1).astype(F32)
    for t in range(4):
        across = jnp.broadcast_to(ranks[t : t + 1], (LANES, LANES))
        down = across.T
        before_ref[t] = jnp.where(down < across, 1.0, 0.0).astype(BF16)
        behind_ref[t] = jnp.where(down > across, 1.0, 0.0).astype(BF16)


def split_dot(value, matrix):
    high = value.astype(BF16)
    low = (value - high.astype(F32)).astype(BF16)
    return jnp.dot(high, matrix, preferred_element_type=F32) + jnp.dot(
        low, matrix, preferred_element_type=F32
    )


RENDER_ROWS = 4
PULL_ROWS = 4


def splat_kernel(
    msg_ref, pix_ref, before_ref, behind_ref, loss_hbm, out_ref,
    turned, places, sources, rows, across, downs, alphas, weights, clear, color, carry, sums, grads,
    loss_ref, sent,
):
    last_part = msg_ref[pl.ds(2, LANES, stride=3), :]
    turned[pl.ds(2 * LANES, LANES), :] = last_part.T
    for b in range(2):
        turned[pl.ds(b * LANES, LANES), :] = msg_ref[pl.ds(b, LANES, stride=3), :].T
    sub = lax.broadcasted_iota(jnp.int32, (8, LANES), 0).astype(F32)
    lane = lax.broadcasted_iota(jnp.int32, (LANES, LANES), 1)
    line = lax.broadcasted_iota(jnp.int32, (LANES, LANES), 0)
    loss_ref[...] = jnp.zeros_like(loss_ref)
    grads[...] = jnp.zeros_like(grads)

    counts = []
    for t in range(4):
        kept = jnp.where(lane[:8] == 0, 1.0, turned[pl.ds(288 + 16 * t + 8, 1), :])
        kept_down = jnp.where(line == 0, 1.0, last_part[:, 32 + 16 * t + 8 : 32 + 16 * t + 9])
        counts.append(jnp.sum(kept[:1]).astype(jnp.int32))
        if t % 2 == 0:
            ahead_of, ahead_down = before_ref[t], behind_ref[t]
        else:
            ahead_of, ahead_down = behind_ref[t], before_ref[t]
        spot = jnp.dot(kept.astype(BF16), ahead_of, preferred_element_type=F32)
        spot_down = jnp.dot(ahead_down, kept_down.astype(BF16), preferred_element_type=F32)
        if t % 2 == 1:
            spot, spot_down = (LANES - 1.0) - spot, (LANES - 1.0) - spot_down
        places[t] = jnp.where(kept > 0.0, spot, -1.0).astype(jnp.int32)
        hit = jnp.logical_and(kept_down > 0.0, spot_down == lane.astype(F32))
        source = jnp.sum(jnp.where(hit, line.astype(F32), 0.0), axis=0, keepdims=True)
        sources[t] = jnp.broadcast_to(source, (8, LANES)).astype(jnp.int32)

    fits = [counts[2 * s] + counts[2 * s + 1] <= LANES for s in range(2)]

    turns = jnp.where(jnp.logical_and(fits[0], fits[1]), 1, 2)
    send = pltpu.make_async_copy(loss_ref, loss_hbm, sent)

    def unit_y(s, k, row):
        return (row.astype(F32) + 0.5 - rows[s, k * 9 + 1]) * rows[s, k * 9 + 3]

    def render(step, unused):
        for s in range(2):
            trans = [[None] * 2 for _ in range(RENDER_ROWS)]
            total = [[[None] * 3 for _ in range(2)] for _ in range(RENDER_ROWS)]
            for k in range(SPLATS):
                shade = [rows[s, k * 9 + 6 + c] for c in range(3)]
                for r in range(RENDER_ROWS):
                    down = unit_y(s, k, step * RENDER_ROWS + r)
                    downs[s, k, step * RENDER_ROWS + r] = down
                    for h in range(2):
                        power = down * (across[s, k, h, 1] - down) - across[s, k, h, 2]
                        alpha = jnp.exp2(power)
                        weight = alpha if k == 0 else trans[r][h] * alpha
                        trans[r][h] = 1.0 - alpha if k == 0 else trans[r][h] - weight
                        alphas[s, k, 2 * (step * RENDER_ROWS + r) + h] = alpha
                        weights[s, k, 2 * (step * RENDER_ROWS + r) + h] = weight
                        for c in range(3):
                            term = weight * shade[c]
                            total[r][h][c] = term if k == 0 else total[r][h][c] + term
            for r in range(RENDER_ROWS):
                for h in range(2):
                    at = pl.ds(pl.multiple_of((step * RENDER_ROWS + r) * 16 + 8 * h, 8), 8)
                    clear[s, at, :] = trans[r][h]
                    for c in range(3):
                        color[s, c, at, :] = total[r][h][c]
        return 0

    def pull(step, unused):
        for s in range(2):
            behind = [None] * (2 * PULL_ROWS)
            slope = [[None] * 3 for _ in range(2 * PULL_ROWS)]
            for n in range(2 * PULL_ROWS):
                at = pl.ds(pl.multiple_of(step * (PULL_ROWS * 16) + 8 * n, 8), 8)
                behind[n] = carry[s, at, :]
                slope[n] = [color[s, c, at, :] for c in range(3)]
            for k in range(SPLATS - 1, -1, -1):
                shade = [rows[s, k * 9 + 6 + c] for c in range(3)]
                acc = [None] * 8

                def add(n, value):
                    acc[n] = value if acc[n] is None else acc[n] + value

                for r in range(PULL_ROWS):
                    down = downs[s, k, step * PULL_ROWS + r]
                    both = None
                    for h in range(2):
                        n = 2 * r + h
                        alpha = alphas[s, k, 2 * PULL_ROWS * step + n]
                        weight = weights[s, k, 2 * PULL_ROWS * step + n]
                        gain = slope[n][0] * shade[0] + slope[n][1] * shade[1] + slope[n][2] * shade[2]
                        change = gain - behind[n]
                        behind[n] = behind[n] + alpha * change
                        pulled = weight * change
                        leaned = pulled * down
                        both = leaned if h == 0 else both + leaned
                        add(2 * h, pulled)
                        add(2 * h + 1, leaned)
                        for c in range(3):
                            add(5 + c, weight * slope[n][c])
                    add(4, both * down)
                for n in range(8):
                    sums[s, k * 8 + n] = sums[s, k * 8 + n] + acc[n]
        return 0

    def constants(s, has_first, has_last):
        t = 2 * s
        flat = lane[:8]
        in_first = flat < jnp.where(has_first, counts[t], 0)
        in_last = flat >= jnp.where(has_last, LANES - counts[t + 1], LANES)
        first_source, last_source = sources[t], sources[t + 1]

        def pick(at, step, empty=0.0):
            left = jnp.take_along_axis(turned[pl.ds(at, 8), :], first_source, axis=1)
            right = jnp.take_along_axis(turned[pl.ds(at + step, 8), :], last_source, axis=1)
            return jnp.where(in_first, left, jnp.where(in_last, right, empty))

        raw = [pick(32 * p + 8 * t, 8) for p in range(9)]
        ranks = pick(288 + 16 * t, 16, sub)
        covered = pick(288 + 16 * t + 8, 16)[:1]
        inv_x = jnp.exp(-raw[2])
        inv_y = jnp.exp(-raw[3])
        curl = jnp.tanh(raw[4])
        rho = 0.9 * curl
        inv_det = 1.0 / (1.0 - rho * rho)
        scale = jnp.sqrt(HALF_LOG2E * inv_det)
        odds = jax.nn.sigmoid(raw[5])
        tint = [jax.nn.sigmoid(raw[6 + c]) for c in range(3)]
        opacity = 0.99 * odds * covered
        faint = jnp.where(opacity > 0.0, jnp.log2(jnp.maximum(opacity, 1.1754944e-38)), -1e30)
        plain = [raw[0], raw[1], inv_x * scale, inv_y * scale, 2.0 * rho, faint] + tint
        return ranks, inv_x, inv_y, curl, rho, inv_det, scale, odds, tint, plain

    def prepare(s, ranks, plain):
        for k in range(SPLATS):
            chosen = ranks == float(k)
            for n, value in enumerate(plain):
                row = jnp.sum(jnp.where(chosen, value, 0.0), axis=0, keepdims=True)
                rows[s, k * 9 + n] = jnp.broadcast_to(row, (8, LANES))
            for h in range(2):
                unit = (sub + (0.5 + 8.0 * h) - rows[s, k * 9]) * rows[s, k * 9 + 2]
                across[s, k, h, 0] = unit
                across[s, k, h, 1] = unit * rows[s, k * 9 + 4]
                across[s, k, h, 2] = unit * unit - rows[s, k * 9 + 5]

    on_lane = lax.broadcasted_iota(jnp.int32, (PIX, LANES), 1)

    def composite(flags):
        borders, logs, sames, rights = [], [], [], []
        for s, (has_first, has_last) in enumerate(flags):
            border = jnp.where(has_first, jnp.where(has_last, counts[2 * s], LANES), 0)
            same = (lane < border) == (line < border)
            left = jnp.where(jnp.logical_and(same, line < lane), 1.0, 0.0).astype(BF16)
            rights.append(jnp.where(jnp.logical_and(same, line > lane), 1.0, 0.0).astype(BF16))
            sames.append(jnp.where(same, 1.0, 0.0).astype(BF16))
            borders.append(border)
            logs.append(split_dot(jnp.log(clear[s]), jnp.concatenate([left, sames[s]], 1)))
        losses = []
        alongs, grad_transes = [], []
        for s in range(2):
            ahead = jnp.exp(logs[s][:, :LANES])
            whole = jnp.exp(logs[s][:, LANES:])
            left_pix = pix_ref[pl.ds(2 * s * PIX, PIX), :]
            right_pix = pix_ref[pl.ds((2 * s + 1) * PIX, PIX), :]
            on_left = on_lane < borders[s]

            def field(n):
                return jnp.where(on_left, left_pix[:, n : n + 1], right_pix[:, n : n + 1])

            inv_square = field(3)
            squares = None
            grad_trans = None
            along = None
            for c in range(3):
                layer = ahead * color[s, c]
                residual = split_dot(layer, sames[s]) + whole - field(c)
                slope = residual * inv_square
                squares = residual * residual if c == 0 else squares + residual * residual
                grad_trans = slope if c == 0 else grad_trans + slope
                along = slope * layer if c == 0 else along + slope * layer
                color[s, c] = ahead * slope
            losses.append(0.5 * squares * inv_square + field(4))
            alongs.append(along)
            grad_transes.append(grad_trans * whole)
        for s, (has_first, has_last) in enumerate(flags):
            follow = split_dot(alongs[s], rights[s]) + grad_transes[s]
            carry[s] = follow / clear[s]
        for s, (has_first, has_last) in enumerate(flags):
            for h in range(2):
                shown = losses[s][h * LANES : (h + 1) * LANES].T
                for here, row, value in (
                    (has_first, 4 * s + h, shown[:1]),
                    (has_last, 4 * s + 2 + h, shown[LANES - 1 :]),
                ):
                    loss_ref[row : row + 1, :] = jnp.where(here, value, loss_ref[row : row + 1, :])

    def finish(s, flag, ranks, inv_x, inv_y, curl, rho, inv_det, scale, odds, tint):
        plain_sums = [None] * 9
        for k in range(SPLATS):
            chosen = ranks == float(k)
            left, right = [[sums[s, k * 8 + 2 * h + n] for n in range(2)] for h in range(2)]
            u0, u1 = across[s, k, 0, 0], across[s, k, 1, 0]
            m0, m1 = left[0] * u0, right[0] * u1
            moments = [
                left[0] + right[0],
                m0 + m1,
                left[1] + right[1],
                m0 * u0 + m1 * u1,
                left[1] * u0 + right[1] * u1,
                sums[s, k * 8 + 4],
            ] + [sums[s, k * 8 + 5 + c] for c in range(3)]
            for n, value in enumerate(moments):
                row = jnp.broadcast_to(jnp.sum(value, axis=0, keepdims=True), (8, LANES))
                plain_sums[n] = (
                    jnp.where(chosen, row, 0.0) if k == 0 else jnp.where(chosen, row, plain_sums[n])
                )
        s0, su, sv, suu, suv, svv = plain_sums[:6]
        inv_scale = 1.0 / scale
        su, sv = su * inv_scale, sv * inv_scale
        inv_both = inv_scale * inv_scale
        suu, suv, svv = suu * inv_both, suv * inv_both, svv * inv_both
        result = [
            inv_det * inv_x * (su - rho * sv),
            inv_det * inv_y * (sv - rho * su),
            inv_det * (suu - rho * suv),
            inv_det * (svv - rho * suv),
            inv_det
            * (suv - rho * inv_det * (suu - 2.0 * rho * suv + svv))
            * (0.9 * (1.0 - curl * curl)),
            s0 * (1.0 - odds),
        ] + [plain_sums[6 + c] * tint[c] * (1.0 - tint[c]) for c in range(3)]
        for here, t in zip(flag, (2 * s, 2 * s + 1)):
            place = places[t]
            taken = jnp.logical_and(place >= 0, here)
            place = jnp.maximum(place, 0)
            for p in range(9):
                at = pl.ds(32 * p + 8 * t, 8)
                value = jnp.take_along_axis(result[p], place, axis=1)
                grads[at, :] = jnp.where(taken, value, grads[at, :])

    def both_blocks(turn, unused):
        opening = turn == 0
        flags = [(opening, jnp.logical_xor(fits[s], turn == 1)) for s in range(2)]
        held = [constants(s, *flags[s]) for s in range(2)]
        for s in range(2):
            prepare(s, held[s][0], held[s][-1])
        lax.fori_loop(0, TSIDE // RENDER_ROWS, render, 0)
        composite(flags)

        @pl.when(turn == turns - 1)
        def _():
            send.start()

        sums[...] = jnp.zeros_like(sums)
        lax.fori_loop(0, TSIDE // PULL_ROWS, pull, 0)
        for s in range(2):
            finish(s, flags[s], *held[s][:-1])
        return 0

    lax.fori_loop(0, turns, both_blocks, 0)
    for b in range(3):
        out_ref[pl.ds(b, LANES, stride=3), :] = grads[pl.ds(b * LANES, LANES), :].T
    send.wait()


def order_matrix(regions):
    levels = regions.bit_length() - 1
    turns = np.zeros((regions - 1, regions), np.float32)
    for r in range(regions):
        for d in range(levels):
            bit = (r >> (levels - 1 - d)) & 1
            turns[2**d - 1 + (r >> (levels - d)), r] = (1 - 2 * bit) * 2 ** (levels - 1 - d)
    return turns


def vmem(*shape, dtype=F32):
    return pltpu.VMEM(shape, dtype)


def shards(gaussians, depth, coverage, flips, features, w_first, b_first, w_second, target):
    regions = lax.axis_size("region")
    my_index = lax.axis_index("region")
    limit = pltpu.CompilerParams(vmem_limit_bytes=32 * 1024 * 1024)

    whole = pltpu.CompilerParams(vmem_limit_bytes=60 * 1024 * 1024)

    def exchange(rows):
        moved = lax.all_to_all(rows.reshape(regions, 1, WIDTH), "region", 0, 0, tiled=True)
        return moved.reshape(rows.shape)

    message = pl.pallas_call(
        pack_kernel,
        out_shape=jax.ShapeDtypeStruct((3 * regions, LANES), F32),
        scratch_shapes=[vmem(512, LANES), vmem(LANES, LANES)],
        compiler_params=whole,
        name="pack",
    )(gaussians.reshape(9, 32, LANES), depth[0].T, coverage)
    received = exchange(message)

    order = jax.ShapeDtypeStruct((4, LANES, LANES), BF16)
    pix, before, behind = pl.pallas_call(
        pixel_kernel,
        in_specs=[pl.BlockSpec(memory_space=pltpu.VMEM)] * 5
        + [pl.BlockSpec(memory_space=pl.ANY), pl.BlockSpec(memory_space=pltpu.VMEM)],
        out_shape=(jax.ShapeDtypeStruct((4 * PIX, LANES), F32), order, order),
        scratch_shapes=[vmem(8, regions - 1, dtype=jnp.int32), pltpu.SemaphoreType.DMA],
        compiler_params=limit,
        cost_estimate=pl.CostEstimate(
            flops=2 * 1024 * 384 * 512, bytes_accessed=2_000_000, transcendentals=1024 * 384
        ),
        name="pixels",
    )(
        features, w_first, b_first, w_second, target, flips,
        jnp.asarray(order_matrix(regions), BF16),
    )

    loss, returned = pl.pallas_call(
        splat_kernel,
        in_specs=[pl.BlockSpec(memory_space=pltpu.VMEM)] * 4,
        out_specs=(pl.BlockSpec(memory_space=pl.ANY), pl.BlockSpec(memory_space=pltpu.VMEM)),
        out_shape=(
            jax.ShapeDtypeStruct((8, LANES), F32),
            jax.ShapeDtypeStruct((3 * regions, LANES), F32),
        ),
        scratch_shapes=[
            vmem(WIDTH, LANES),
            vmem(4, 8, LANES, dtype=jnp.int32),
            vmem(4, 8, LANES, dtype=jnp.int32),
            vmem(2, 72, 8, LANES),
            vmem(2, SPLATS, 2, 3, 8, LANES),
            vmem(2, SPLATS, TSIDE, 8, LANES),
            vmem(2, SPLATS, PIX // 8, 8, LANES),
            vmem(2, SPLATS, PIX // 8, 8, LANES),
            vmem(2, PIX, LANES),
            vmem(2, 3, PIX, LANES),
            vmem(2, PIX, LANES),
            vmem(2, 64, 8, LANES),
            vmem(WIDTH, LANES),
            vmem(8, LANES),
            pltpu.SemaphoreType.DMA,
        ],
        compiler_params=limit,
        name="splats",
    )(received, pix, before, behind)

    back = exchange(returned)
    splat_grads = pl.pallas_call(
        unpack_kernel,
        out_shape=jax.ShapeDtypeStruct((9, 32, LANES), F32),
        compiler_params=limit,
        name="unpack",
    )(back)
    return loss.reshape(4 * PIX), splat_grads.reshape(1, 9, 32 * LANES)


def solution(mesh):
    placed = (
        P("region", None, None),
        P("region", None, None),
        P("region", None),
        P(),
        P("region", None),
        P(),
        P(),
        P(),
        P(None, "region"),
    )
    return jax.shard_map(
        shards,
        mesh=mesh,
        in_specs=placed,
        out_specs=(P("region"), P("region", None, None)),
        check_vma=False,
    )
```

```python
import math

import jax
import jax.numpy as jnp
import numpy as np
from jax import lax
from jax.experimental import pallas as pl
from jax.experimental.pallas import tpu as pltpu
from jax.sharding import PartitionSpec as P

TSIDE = 16
PIX = TSIDE * TSIDE
SPLATS = 8
LANES = 128
WIDTH = 384
HALF_LOG2E = 0.5 * math.log2(math.e)
F32 = jnp.float32
BF16 = jnp.bfloat16


def cut_columns(source, shift):
    return pltpu.roll(source, shift, 1) if shift else source


def pack_kernel(gauss_ref, depth_ref, cover_ref, out_ref, turned, strided):
    group = lax.broadcasted_iota(jnp.int32, (32, LANES), 1) // 32
    for part in range(3):
        for d in range(4):
            block = None
            for a in range(min(4, 9 - 4 * part)):
                moved = cut_columns(gauss_ref[4 * part + a], 32 * ((a - d) % 4))
                block = moved if block is None else jnp.where(group == a, moved, block)
            if part < 2:
                out_ref[pl.ds(3 * d + part, 32, stride=12), :] = block
            else:
                strided[pl.ds(d, 32, stride=4), :] = block
    ranks = depth_ref[...].astype(F32)
    covered = cover_ref[...].astype(F32)
    filler = jnp.zeros((LANES - 16, 512), F32)
    row = lax.broadcasted_iota(jnp.int32, (8, 512), 0)
    covered = jnp.where(row == 0, jnp.broadcast_to(covered, (8, 512)), 0.0)
    stacked = jnp.concatenate([ranks, covered, filler], 0)
    for b in range(4):
        turned[pl.ds(b * LANES, LANES), :] = stacked[:, b * LANES : (b + 1) * LANES].T
    tail = None
    for t in range(4):
        moved = pltpu.roll(turned[pl.ds(t, LANES, stride=4), :], 32 + 16 * t, 1)
        tail = moved if tail is None else tail + moved
    lane = lax.broadcasted_iota(jnp.int32, (LANES, LANES), 1)
    out_ref[pl.ds(2, LANES, stride=3), :] = jnp.where(lane < 32, strided[...], tail)


def unpack_kernel(msg_ref, out_ref):
    group = lax.broadcasted_iota(jnp.int32, (32, LANES), 1) // 32
    for p in range(9):
        a, part = p % 4, p // 4
        block = None
        for d in range(4):
            moved = cut_columns(msg_ref[pl.ds(3 * d + part, 32, stride=12), :], 32 * ((d - a) % 4))
            block = moved if block is None else jnp.where(group == d, moved, block)
        out_ref[p] = block


def pixel_kernel(
    feat_ref, w_first_ref, b_first_ref, w_second_ref, target_ref, flips_hbm, turns_ref,
    pix_ref, before_ref, behind_ref, flipped, arrived,
):
    me = lax.axis_index("region")
    first_row = pl.multiple_of(8 * (me // 2), 8)
    fetch = pltpu.make_async_copy(flips_hbm.at[pl.ds(first_row, 8), :], flipped, arrived)
    fetch.start()
    rows = jnp.broadcast_to(w_second_ref[...][None, :], (16, w_second_ref.shape[0]))
    filler = jnp.zeros((LANES - 8, PIX), F32)
    row = lax.broadcasted_iota(jnp.int32, (8, PIX), 0)
    bias = b_first_ref[...][None, :]
    for t in range(4):
        at = pl.ds(t * PIX, PIX)
        pre = jnp.dot(feat_ref[at, :], w_first_ref[...], preferred_element_type=F32) + bias
        hidden = jax.nn.gelu(pre).astype(BF16)
        score = lax.dot_general(
            rows, hidden, (((1,), (1,)), ((), ())), preferred_element_type=F32
        )[:8]
        spread = 0.5 + (jnp.maximum(score, 0.0) + jnp.log1p(jnp.exp(-jnp.abs(score))))
        rest = jnp.where(row == 3, 1.0 / (spread * spread), jnp.log(spread))
        wanted = target_ref[:, t * PIX : (t + 1) * PIX]
        for c in range(3):
            rest = jnp.where(row == c, wanted[c : c + 1], rest)
        pix_ref[at, :] = jnp.concatenate([rest, filler], 0).T
    fetch.wait()
    turned = jnp.dot(
        flipped[...].astype(F32).astype(BF16), turns_ref[...], preferred_element_type=F32
    )
    ranks = jnp.where(me % 2 == 0, turned[:4], turned[4:])
    ranks = ranks + lax.broadcasted_iota(jnp.int32, (4, LANES), 1).astype(F32)
    for t in range(4):
        across = jnp.broadcast_to(ranks[t : t + 1], (LANES, LANES))
        down = across.T
        before_ref[t] = jnp.where(down < across, 1.0, 0.0).astype(BF16)
        behind_ref[t] = jnp.where(down > across, 1.0, 0.0).astype(BF16)


def split_dot(value, matrix):
    high = value.astype(BF16)
    low = (value - high.astype(F32)).astype(BF16)
    return jnp.dot(high, matrix, preferred_element_type=F32) + jnp.dot(
        low, matrix, preferred_element_type=F32
    )


RENDER_ROWS = 4
PULL_ROWS = 4


def splat_kernel(
    msg_ref, pix_ref, before_ref, behind_ref, loss_hbm, out_ref,
    turned, places, sources, rows, across, downs, alphas, weights, clear, color, carry, sums, grads,
    loss_ref, sent,
):
    last_part = msg_ref[pl.ds(2, LANES, stride=3), :]
    turned[pl.ds(2 * LANES, LANES), :] = last_part.T
    for b in range(2):
        turned[pl.ds(b * LANES, LANES), :] = msg_ref[pl.ds(b, LANES, stride=3), :].T
    sub = lax.broadcasted_iota(jnp.int32, (8, LANES), 0).astype(F32)
    lane = lax.broadcasted_iota(jnp.int32, (LANES, LANES), 1)
    line = lax.broadcasted_iota(jnp.int32, (LANES, LANES), 0)
    loss_ref[...] = jnp.zeros_like(loss_ref)
    grads[...] = jnp.zeros_like(grads)

    counts = []
    for t in range(4):
        kept = jnp.where(lane[:8] == 0, 1.0, turned[pl.ds(288 + 16 * t + 8, 1), :])
        kept_down = jnp.where(line == 0, 1.0, last_part[:, 32 + 16 * t + 8 : 32 + 16 * t + 9])
        counts.append(jnp.sum(kept[:1]).astype(jnp.int32))
        if t % 2 == 0:
            ahead_of, ahead_down = before_ref[t], behind_ref[t]
        else:
            ahead_of, ahead_down = behind_ref[t], before_ref[t]
        spot = jnp.dot(kept.astype(BF16), ahead_of, preferred_element_type=F32)
        spot_down = jnp.dot(ahead_down, kept_down.astype(BF16), preferred_element_type=F32)
        if t % 2 == 1:
            spot, spot_down = (LANES - 1.0) - spot, (LANES - 1.0) - spot_down
        places[t] = jnp.where(kept > 0.0, spot, -1.0).astype(jnp.int32)
        hit = jnp.logical_and(kept_down > 0.0, spot_down == lane.astype(F32))
        source = jnp.sum(jnp.where(hit, line.astype(F32), 0.0), axis=0, keepdims=True)
        sources[t] = jnp.broadcast_to(source, (8, LANES)).astype(jnp.int32)

    fits = [counts[2 * s] + counts[2 * s + 1] <= LANES for s in range(2)]

    turns = jnp.where(jnp.logical_and(fits[0], fits[1]), 1, 2)
    send = pltpu.make_async_copy(loss_ref, loss_hbm, sent)

    def unit_y(s, k, row):
        return (row.astype(F32) + 0.5 - rows[s, k * 9 + 1]) * rows[s, k * 9 + 3]

    def render(step, unused):
        for s in range(2):
            trans = [[None] * 2 for _ in range(RENDER_ROWS)]
            total = [[[None] * 3 for _ in range(2)] for _ in range(RENDER_ROWS)]
            for k in range(SPLATS):
                shade = [rows[s, k * 9 + 6 + c] for c in range(3)]
                for r in range(RENDER_ROWS):
                    down = unit_y(s, k, step * RENDER_ROWS + r)
                    downs[s, k, step * RENDER_ROWS + r] = down
                    for h in range(2):
                        power = down * (across[s, k, h, 1] - down) - across[s, k, h, 2]
                        alpha = jnp.exp2(power)
                        weight = alpha if k == 0 else trans[r][h] * alpha
                        trans[r][h] = 1.0 - alpha if k == 0 else trans[r][h] - weight
                        alphas[s, k, 2 * (step * RENDER_ROWS + r) + h] = alpha
                        weights[s, k, 2 * (step * RENDER_ROWS + r) + h] = weight
                        for c in range(3):
                            term = weight * shade[c]
                            total[r][h][c] = term if k == 0 else total[r][h][c] + term
            for r in range(RENDER_ROWS):
                for h in range(2):
                    at = pl.ds(pl.multiple_of((step * RENDER_ROWS + r) * 16 + 8 * h, 8), 8)
                    clear[s, at, :] = trans[r][h]
                    for c in range(3):
                        color[s, c, at, :] = total[r][h][c]
        return 0

    def pull(step, unused):
        for s in range(2):
            behind = [None] * (2 * PULL_ROWS)
            slope = [[None] * 3 for _ in range(2 * PULL_ROWS)]
            for n in range(2 * PULL_ROWS):
                at = pl.ds(pl.multiple_of(step * (PULL_ROWS * 16) + 8 * n, 8), 8)
                behind[n] = carry[s, at, :]
                slope[n] = [color[s, c, at, :] for c in range(3)]
            for k in range(SPLATS - 1, -1, -1):
                shade = [rows[s, k * 9 + 6 + c] for c in range(3)]
                acc = [None] * 8

                def add(n, value):
                    acc[n] = value if acc[n] is None else acc[n] + value

                for r in range(PULL_ROWS):
                    down = downs[s, k, step * PULL_ROWS + r]
                    both = None
                    for h in range(2):
                        n = 2 * r + h
                        alpha = alphas[s, k, 2 * PULL_ROWS * step + n]
                        weight = weights[s, k, 2 * PULL_ROWS * step + n]
                        gain = slope[n][0] * shade[0] + slope[n][1] * shade[1] + slope[n][2] * shade[2]
                        change = gain - behind[n]
                        behind[n] = behind[n] + alpha * change
                        pulled = weight * change
                        leaned = pulled * down
                        both = leaned if h == 0 else both + leaned
                        add(2 * h, pulled)
                        add(2 * h + 1, leaned)
                        for c in range(3):
                            add(5 + c, weight * slope[n][c])
                    add(4, both * down)
                for n in range(8):
                    sums[s, k * 8 + n] = sums[s, k * 8 + n] + acc[n]
        return 0

    def constants(s, has_first, has_last):
        t = 2 * s
        flat = lane[:8]
        in_first = flat < jnp.where(has_first, counts[t], 0)
        in_last = flat >= jnp.where(has_last, LANES - counts[t + 1], LANES)
        first_source, last_source = sources[t], sources[t + 1]

        def pick(at, step, empty=0.0):
            left = jnp.take_along_axis(turned[pl.ds(at, 8), :], first_source, axis=1)
            right = jnp.take_along_axis(turned[pl.ds(at + step, 8), :], last_source, axis=1)
            return jnp.where(in_first, left, jnp.where(in_last, right, empty))

        raw = [pick(32 * p + 8 * t, 8) for p in range(9)]
        ranks = pick(288 + 16 * t, 16, sub)
        covered = pick(288 + 16 * t + 8, 16)[:1]
        inv_x = jnp.exp(-raw[2])
        inv_y = jnp.exp(-raw[3])
        curl = jnp.tanh(raw[4])
        rho = 0.9 * curl
        inv_det = 1.0 / (1.0 - rho * rho)
        scale = jnp.sqrt(HALF_LOG2E * inv_det)
        odds = jax.nn.sigmoid(raw[5])
        tint = [jax.nn.sigmoid(raw[6 + c]) for c in range(3)]
        opacity = 0.99 * odds * covered
        faint = jnp.where(opacity > 0.0, jnp.log2(jnp.maximum(opacity, 1.1754944e-38)), -1e30)
        plain = [raw[0], raw[1], inv_x * scale, inv_y * scale, 2.0 * rho, faint] + tint
        return ranks, inv_x, inv_y, curl, rho, inv_det, scale, odds, tint, plain

    def prepare(s, ranks, plain):
        order = jnp.zeros((8, LANES), F32)
        for g in range(1, SPLATS):
            order = jnp.where(ranks[g : g + 1] == sub, float(g), order)
        order = order.astype(jnp.int32)
        plain = [jnp.take_along_axis(value, order, axis=0) for value in plain]
        for k in range(SPLATS):
            for n, value in enumerate(plain):
                rows[s, k * 9 + n] = jnp.broadcast_to(value[k : k + 1], (8, LANES))
            for h in range(2):
                unit = (sub + (0.5 + 8.0 * h) - rows[s, k * 9]) * rows[s, k * 9 + 2]
                across[s, k, h, 0] = unit
                across[s, k, h, 1] = unit * rows[s, k * 9 + 4]
                across[s, k, h, 2] = unit * unit - rows[s, k * 9 + 5]

    on_lane = lax.broadcasted_iota(jnp.int32, (PIX, LANES), 1)

    def composite(flags):
        borders, logs, sames, rights = [], [], [], []
        for s, (has_first, has_last) in enumerate(flags):
            border = jnp.where(has_first, jnp.where(has_last, counts[2 * s], LANES), 0)
            same = (lane < border) == (line < border)
            left = jnp.where(jnp.logical_and(same, line < lane), 1.0, 0.0).astype(BF16)
            rights.append(jnp.where(jnp.logical_and(same, line > lane), 1.0, 0.0).astype(BF16))
            sames.append(jnp.where(same, 1.0, 0.0).astype(BF16))
            borders.append(border)
            logs.append(split_dot(jnp.log(clear[s]), jnp.concatenate([left, sames[s]], 1)))
        losses = []
        alongs, grad_transes = [], []
        for s in range(2):
            ahead = jnp.exp(logs[s][:, :LANES])
            whole = jnp.exp(logs[s][:, LANES:])
            left_pix = pix_ref[pl.ds(2 * s * PIX, PIX), :]
            right_pix = pix_ref[pl.ds((2 * s + 1) * PIX, PIX), :]
            on_left = on_lane < borders[s]

            def field(n):
                return jnp.where(on_left, left_pix[:, n : n + 1], right_pix[:, n : n + 1])

            inv_square = field(3)
            squares = None
            grad_trans = None
            along = None
            for c in range(3):
                layer = ahead * color[s, c]
                residual = split_dot(layer, sames[s]) + whole - field(c)
                slope = residual * inv_square
                squares = residual * residual if c == 0 else squares + residual * residual
                grad_trans = slope if c == 0 else grad_trans + slope
                along = slope * layer if c == 0 else along + slope * layer
                color[s, c] = ahead * slope
            losses.append(0.5 * squares * inv_square + field(4))
            alongs.append(along)
            grad_transes.append(grad_trans * whole)
        for s, (has_first, has_last) in enumerate(flags):
            follow = split_dot(alongs[s], rights[s]) + grad_transes[s]
            carry[s] = follow / clear[s]
        for s, (has_first, has_last) in enumerate(flags):
            for h in range(2):
                shown = losses[s][h * LANES : (h + 1) * LANES].T
                for here, row, value in (
                    (has_first, 4 * s + h, shown[:1]),
                    (has_last, 4 * s + 2 + h, shown[LANES - 1 :]),
                ):
                    loss_ref[row : row + 1, :] = jnp.where(here, value, loss_ref[row : row + 1, :])

    def finish(s, flag, ranks, inv_x, inv_y, curl, rho, inv_det, scale, odds, tint):
        plain_sums = [None] * 9
        for k in range(SPLATS):
            chosen = ranks == float(k)
            left, right = [[sums[s, k * 8 + 2 * h + n] for n in range(2)] for h in range(2)]
            u0, u1 = across[s, k, 0, 0], across[s, k, 1, 0]
            m0, m1 = left[0] * u0, right[0] * u1
            moments = [
                left[0] + right[0],
                m0 + m1,
                left[1] + right[1],
                m0 * u0 + m1 * u1,
                left[1] * u0 + right[1] * u1,
                sums[s, k * 8 + 4],
            ] + [sums[s, k * 8 + 5 + c] for c in range(3)]
            for n, value in enumerate(moments):
                row = jnp.broadcast_to(jnp.sum(value, axis=0, keepdims=True), (8, LANES))
                plain_sums[n] = (
                    jnp.where(chosen, row, 0.0) if k == 0 else jnp.where(chosen, row, plain_sums[n])
                )
        s0, su, sv, suu, suv, svv = plain_sums[:6]
        inv_scale = 1.0 / scale
        su, sv = su * inv_scale, sv * inv_scale
        inv_both = inv_scale * inv_scale
        suu, suv, svv = suu * inv_both, suv * inv_both, svv * inv_both
        result = [
            inv_det * inv_x * (su - rho * sv),
            inv_det * inv_y * (sv - rho * su),
            inv_det * (suu - rho * suv),
            inv_det * (svv - rho * suv),
            inv_det
            * (suv - rho * inv_det * (suu - 2.0 * rho * suv + svv))
            * (0.9 * (1.0 - curl * curl)),
            s0 * (1.0 - odds),
        ] + [plain_sums[6 + c] * tint[c] * (1.0 - tint[c]) for c in range(3)]
        for here, t in zip(flag, (2 * s, 2 * s + 1)):
            place = places[t]
            taken = jnp.logical_and(place >= 0, here)
            place = jnp.maximum(place, 0)
            for p in range(9):
                at = pl.ds(32 * p + 8 * t, 8)
                value = jnp.take_along_axis(result[p], place, axis=1)
                grads[at, :] = jnp.where(taken, value, grads[at, :])

    def both_blocks(turn, unused):
        opening = turn == 0
        flags = [(opening, jnp.logical_xor(fits[s], turn == 1)) for s in range(2)]
        held = [constants(s, *flags[s]) for s in range(2)]
        for s in range(2):
            prepare(s, held[s][0], held[s][-1])
        lax.fori_loop(0, TSIDE // RENDER_ROWS, render, 0)
        composite(flags)

        @pl.when(turn == turns - 1)
        def _():
            send.start()

        sums[...] = jnp.zeros_like(sums)
        lax.fori_loop(0, TSIDE // PULL_ROWS, pull, 0)
        for s in range(2):
            finish(s, flags[s], *held[s][:-1])
        return 0

    lax.fori_loop(0, turns, both_blocks, 0)
    for b in range(3):
        out_ref[pl.ds(b, LANES, stride=3), :] = grads[pl.ds(b * LANES, LANES), :].T
    send.wait()


def order_matrix(regions):
    levels = regions.bit_length() - 1
    turns = np.zeros((regions - 1, regions), np.float32)
    for r in range(regions):
        for d in range(levels):
            bit = (r >> (levels - 1 - d)) & 1
            turns[2**d - 1 + (r >> (levels - d)), r] = (1 - 2 * bit) * 2 ** (levels - 1 - d)
    return turns


def vmem(*shape, dtype=F32):
    return pltpu.VMEM(shape, dtype)


def shards(gaussians, depth, coverage, flips, features, w_first, b_first, w_second, target):
    regions = lax.axis_size("region")
    my_index = lax.axis_index("region")
    limit = pltpu.CompilerParams(vmem_limit_bytes=32 * 1024 * 1024)

    whole = pltpu.CompilerParams(vmem_limit_bytes=60 * 1024 * 1024)

    def exchange(rows):
        moved = lax.all_to_all(rows.reshape(regions, 1, WIDTH), "region", 0, 0, tiled=True)
        return moved.reshape(rows.shape)

    message = pl.pallas_call(
        pack_kernel,
        out_shape=jax.ShapeDtypeStruct((3 * regions, LANES), F32),
        scratch_shapes=[vmem(512, LANES), vmem(LANES, LANES)],
        compiler_params=whole,
        name="pack",
    )(gaussians.reshape(9, 32, LANES), depth[0].T, coverage)
    received = exchange(message)

    order = jax.ShapeDtypeStruct((4, LANES, LANES), BF16)
    pix, before, behind = pl.pallas_call(
        pixel_kernel,
        in_specs=[pl.BlockSpec(memory_space=pltpu.VMEM)] * 5
        + [pl.BlockSpec(memory_space=pl.ANY), pl.BlockSpec(memory_space=pltpu.VMEM)],
        out_shape=(jax.ShapeDtypeStruct((4 * PIX, LANES), F32), order, order),
        scratch_shapes=[vmem(8, regions - 1, dtype=jnp.int32), pltpu.SemaphoreType.DMA],
        compiler_params=limit,
        cost_estimate=pl.CostEstimate(
            flops=2 * 1024 * 384 * 512, bytes_accessed=2_000_000, transcendentals=1024 * 384
        ),
        name="pixels",
    )(
        features, w_first, b_first, w_second, target, flips,
        jnp.asarray(order_matrix(regions), BF16),
    )

    loss, returned = pl.pallas_call(
        splat_kernel,
        in_specs=[pl.BlockSpec(memory_space=pltpu.VMEM)] * 4,
        out_specs=(pl.BlockSpec(memory_space=pl.ANY), pl.BlockSpec(memory_space=pltpu.VMEM)),
        out_shape=(
            jax.ShapeDtypeStruct((8, LANES), F32),
            jax.ShapeDtypeStruct((3 * regions, LANES), F32),
        ),
        scratch_shapes=[
            vmem(WIDTH, LANES),
            vmem(4, 8, LANES, dtype=jnp.int32),
            vmem(4, 8, LANES, dtype=jnp.int32),
            vmem(2, 72, 8, LANES),
            vmem(2, SPLATS, 2, 3, 8, LANES),
            vmem(2, SPLATS, TSIDE, 8, LANES),
            vmem(2, SPLATS, PIX // 8, 8, LANES),
            vmem(2, SPLATS, PIX // 8, 8, LANES),
            vmem(2, PIX, LANES),
            vmem(2, 3, PIX, LANES),
            vmem(2, PIX, LANES),
            vmem(2, 64, 8, LANES),
            vmem(WIDTH, LANES),
            vmem(8, LANES),
            pltpu.SemaphoreType.DMA,
        ],
        compiler_params=limit,
        name="splats",
    )(received, pix, before, behind)

    back = exchange(returned)
    splat_grads = pl.pallas_call(
        unpack_kernel,
        out_shape=jax.ShapeDtypeStruct((9, 32, LANES), F32),
        compiler_params=limit,
        name="unpack",
    )(back)
    return loss.reshape(4 * PIX), splat_grads.reshape(1, 9, 32 * LANES)


def solution(mesh):
    placed = (
        P("region", None, None),
        P("region", None, None),
        P("region", None),
        P(),
        P("region", None),
        P(),
        P(),
        P(),
        P(None, "region"),
    )
    return jax.shard_map(
        shards,
        mesh=mesh,
        in_specs=placed,
        out_specs=(P("region"), P("region", None, None)),
        check_vma=False,
    )
```
